256 devices in a mesh: ctx: 16 (over x_lo, z), tp: 16 (over y, x_hi, core).
Axes of the slice: x: 4 (x_hi: 2, x_lo: 2; x = x_hi * 2 + x_lo), y: 4, z: 8, core: 2. Of those that a mesh axis runs over, the one named last changes fastest.
Arguments:
- queries: bfloat16 [1024, 128, 128], P('ctx', 'tp'), may hold values from -400 to 400
- cache_keys: bfloat16 [8, 32768, 128], P(None, 'ctx'), may hold values from -6 to 6
- cache_values: bfloat16 [8, 32768, 128], P(None, 'ctx'), may hold values from -12 to 12
- span_keys: bfloat16 [8, 1024, 128], P(None, 'ctx'), may hold values from -3.6 to 3.6
- span_values: bfloat16 [8, 1024, 128], P(None, 'ctx'), may hold values from -12 to 12
- span_start: int32 [1], replicated, may hold values from 8192 to 15360
- cache_lengths: int32 [16], P('ctx'), may hold values from 1 to 2048, 16384 in all
- out_weight: bfloat16 [16384, 16384], P('tp', 'ctx'), may hold values from -0.046875 to 0.046875
Outputs:
- attended: bfloat16 [1024, 128, 128], P('ctx', 'tp')
- projected: bfloat16 [1024, 16384], P('tp', 'ctx')
The draws below stay inside these ranges and needn't reach their ends.
All inputs are finite; a program needn't handle non-finite values. No bound on the sum of `cache_lengths` on one device may be relied on, other than what follows from the above.
Results may differ from the reference program's by a relative error of at most 0.019.
Values may be sent and summed in bfloat16 or wider, within the bound.
No kernel may reach another device: no remote copies, remote signals or barrier semaphores. Data moves between devices by JAX's collectives and lax.ppermute only.
A program may use at most 128 MiB of HBM per device.

```python
import math
import jax
import jax.numpy as jnp
import numpy as np
from jax import lax

D = 16384
H = 128
KVH = 8
HD = 128
L_DEV = 2048
SPAN = 1024
CTX_LEN = 32768
N_CTX = 16
N_TP = 16


def draw_span_keys(key, part):
    key = jax.random.fold_in(key, 11)
    sample = jnp.clip(jax.random.normal(key, (KVH, SPAN, HD), jnp.float32), -3.5, 3.5)
    return sample.astype(jnp.bfloat16)


def draw_queries(key, part):
    key = jax.random.fold_in(key, 23)
    sample = jnp.clip(jax.random.normal(key, (SPAN, H, HD), jnp.float32), -3.5, 3.5)
    return sample.astype(jnp.bfloat16)


def draw_cache_values(key, part):
    key = jax.random.fold_in(key, 37)
    shard_key = jax.random.fold_in(key, 1)
    noise_key = jax.random.fold_in(key, 2)
    shard_count = CTX_LEN // L_DEV
    level = 2.5 * jnp.clip(jax.random.normal(shard_key, (KVH, shard_count, 1, HD), jnp.float32), -3.0, 3.0)
    noise = jnp.clip(jax.random.normal(noise_key, (KVH, shard_count, L_DEV, HD), jnp.float32), -3.0, 3.0)
    sample = (level + noise).reshape(KVH, CTX_LEN, HD)
    return sample.astype(jnp.bfloat16)


def level_of(rng, shape, pieces, low, top_value):
    factor_of = 1.0
    for dim, shards_of in pieces:
        draws = jax.random.uniform(jax.random.fold_in(jax.random.fold_in(rng, 6), dim), (shards_of,), jnp.float32, low / len(pieces), top_value / len(pieces))
        factor_of = factor_of * jnp.repeat(jnp.exp(draws), shape[dim] // shards_of).reshape((-1,) + (1,) * (len(shape) - 1 - dim))
    return factor_of


def profile(number_of, total, bound, slope):
    loads = [(1 << 20) // math.isqrt(grade ** slope) + 1 for grade in range(2, number_of + 1)]
    spare, counts = total - bound - (number_of - 1), [1] * (number_of - 1)
    while spare > 0:
        movable = [i for i in range(number_of - 1) if counts[i] < bound]
        mass, left = sum([loads[i] for i in movable]), spare
        for i in movable:
            addition = min(bound - counts[i], max(1, left * loads[i] // mass), spare)
            counts[i] = counts[i] + addition
            spare = spare - addition
    return np.array([bound] + counts)


def ragged(key, number_of, total, limit, slope):
    if number_of == 2:
        one = jax.random.randint(key, (), max(1, total - limit), min(limit, total - 1) + 1)
        return jnp.stack([one, total - one])
    sizes = jnp.asarray(profile(number_of, total, limit, slope), jnp.int32)
    twos = (number_of - 1) // 2
    giver, receiver = sizes[1:1 + 2 * twos:2], sizes[2:2 + 2 * twos:2]
    margin = jnp.minimum(giver - 1, limit - receiver)
    shifted = jax.random.randint(jax.random.fold_in(key, 1), (twos,), 0, 1 << 20) % (margin + 1)
    sizes = sizes.at[1:1 + 2 * twos:2].set(giver - shifted).at[2:2 + 2 * twos:2].set(receiver + shifted)
    return sizes[jax.random.permutation(jax.random.fold_in(key, 2), number_of)]


def centred(own_key, dims, deviation, bound, shards=(), held_as=jnp.bfloat16):
    values = jax.random.normal(own_key, dims, jnp.float32) * deviation
    if len(shards) > 0:
        values = level_of(own_key, dims, shards, -0.22, 0.18) * values
    return jnp.clip(values, min=-bound, max=bound).astype(held_as)


def setup_inputs(seed: int = 0) -> dict:
    seeds = jax.random.split(jax.random.key(seed), 9)
    queries = draw_queries(jax.random.fold_in(seeds[8], 71), 0)
    cache_keys = centred(seeds[1], (KVH, CTX_LEN, HD), 1.0, 6.0, ((1, 16),))
    cache_values = draw_cache_values(jax.random.fold_in(seeds[8], 71), 0)
    span_keys = draw_span_keys(jax.random.fold_in(seeds[8], 71), 0)
    span_values = centred(seeds[4], (KVH, SPAN, HD), 3.0, 12.0, ((1, 16),))
    span_start = jax.random.randint(seeds[5], (1,), N_CTX * L_DEV // 4, N_CTX * L_DEV // 2 - L_DEV // 2 + 1).astype(jnp.int32)
    cache_lengths = ragged(seeds[6], N_CTX, N_CTX * L_DEV // 2, L_DEV, 0).astype(jnp.int32)
    out_weight = centred(seeds[7], (H * HD, D), (H * HD) ** -0.5, 0.046875, ((0, 16), (1, 16)))
    return dict(queries=queries, cache_keys=cache_keys, cache_values=cache_values, span_keys=span_keys, span_values=span_values, span_start=span_start, cache_lengths=cache_lengths, out_weight=out_weight)


NEG_FILL = -1e30


def reference(queries, cache_keys, cache_values, span_keys, span_values, span_start, cache_lengths, out_weight):
    group_size = H // KVH
    score_scale = HD ** -0.5
    start_pos = span_start[0]
    offsets = jnp.cumsum(cache_lengths) - cache_lengths
    slot_index = jnp.arange(L_DEV, dtype=jnp.int32)
    cache_allowed = ((slot_index[None, :] < cache_lengths[:, None]) & (offsets[:, None] + slot_index[None, :] < start_pos)).reshape(CTX_LEN)
    key_table = jnp.concatenate([cache_keys, span_keys], axis=1).astype(jnp.float32)
    value_table = jnp.concatenate([cache_values, span_values], axis=1).astype(jnp.float32)
    block_rows = min(128, SPAN)
    block_count = SPAN // block_rows
    grouped = queries.reshape(block_count, block_rows, KVH, group_size, HD).astype(jnp.float32)
    span_index = jnp.arange(SPAN, dtype=jnp.int32)

    def one_block(inputs):
        query_block, row_first = inputs
        row_index = row_first + jnp.arange(block_rows, dtype=jnp.int32)
        own_allowed = span_index[None, :] <= row_index[:, None]
        allowed = jnp.concatenate([jnp.broadcast_to(cache_allowed[None, :], (block_rows, CTX_LEN)), own_allowed], axis=1)

        def one_head(head_inputs):
            head_query, head_keys, head_values = head_inputs
            scores = jnp.einsum("tgd,kd->tgk", head_query, head_keys) * score_scale
            scores = jnp.where(allowed[:, None, :], scores, NEG_FILL)
            row_peak = jnp.max(scores, axis=-1, keepdims=True)
            weights = jnp.where(allowed[:, None, :], jnp.exp(scores - row_peak), 0.0)
            totals = jnp.sum(weights, axis=-1)
            rounded = lax.optimization_barrier(weights.astype(jnp.bfloat16)).astype(jnp.float32)
            mixed_values = jnp.einsum("tgk,kd->tgd", rounded, head_values)
            return (mixed_values / totals[..., None]).astype(jnp.bfloat16)

        per_head = lax.map(one_head, (jnp.transpose(query_block, (1, 0, 2, 3)), key_table, value_table))
        return jnp.transpose(per_head, (1, 0, 2, 3)).reshape(block_rows, H, HD)

    firsts = jnp.arange(block_count, dtype=jnp.int32) * block_rows
    attended = lax.map(one_block, (grouped, firsts)).reshape(SPAN, H, HD)
    width_dev = H * HD // N_TP
    flat_rows = attended.reshape(SPAN, N_TP, width_dev).transpose(1, 0, 2)
    weight_parts = out_weight.reshape(N_TP, width_dev, D)

    def add_part(running_sum, part_inputs):
        rows_part, weight_part = part_inputs
        partial_term = jnp.dot(rows_part, weight_part, preferred_element_type=jnp.float32)
        return running_sum + lax.optimization_barrier(partial_term.astype(jnp.bfloat16)).astype(jnp.float32), None

    running_sum, ignored = lax.scan(add_part, jnp.zeros((SPAN, D), jnp.float32), (flat_rows, weight_parts))
    return attended, running_sum.astype(jnp.bfloat16)
```

```python
import functools
import math

import jax
import jax.numpy as jnp
from jax import lax
from jax.experimental import pallas as pl
from jax.experimental.pallas import tpu as pltpu
from jax.sharding import Mesh, PartitionSpec as P

H = 128
KVH = 8
HD = 128
NEG = -1e30
C2 = math.log2(math.e) / math.sqrt(HD)
TILE = 512
ROWS = 512
STAT = 32
NZ = 8
SAFE = 90.0
F32 = jnp.float32
BF16 = jnp.bfloat16
MB = 1024 * 1024


def eye_mask():
    r = lax.broadcasted_iota(jnp.int32, (128, 128), 0)
    c = lax.broadcasted_iota(jnp.int32, (128, 128), 1)
    return r == c


def split3(x):
    hi = x.astype(BF16)
    rest = x - hi.astype(F32)
    mid = rest.astype(BF16)
    lo = (rest - mid.astype(F32)).astype(BF16)
    return hi, mid, lo


def pack_kernel(place, ck, cv, sk, sv, near_out, far_out, rest_out, sem):
    core, kv = place[0], place[2]
    n = ck.shape[1]

    def copies(cache, span, out, head, first):
        return [
            pltpu.make_async_copy(cache.at[head], out.at[pl.ds(0, n)], sem.at[first]),
            pltpu.make_async_copy(span.at[head], out.at[pl.ds(n, 64)], sem.at[first + 1]),
        ]

    def move(cache, span, cache2, span2):
        mine = copies(cache, span, far_out, kv ^ 1, 0) + copies(cache, span, near_out, kv, 2)
        mine += copies(cache2, span2, rest_out, kv, 4)
        for c in mine:
            c.start()
        for c in mine:
            c.wait()

    pl.when(core == 0)(lambda: move(ck, sk, cv, sv))
    pl.when(core == 1)(lambda: move(cv, sv, ck, sk))


def pack(place, ck, cv, sk, sv):
    n = ck.shape[1] + 64
    shape = jax.ShapeDtypeStruct((n, HD), BF16)
    return pl.pallas_call(
        pack_kernel,
        out_shape=[shape] * 3,
        in_specs=[pl.BlockSpec(memory_space=pltpu.SMEM)] + [pl.BlockSpec(memory_space=pl.ANY)] * 4,
        out_specs=[pl.BlockSpec(memory_space=pltpu.VMEM)] * 3,
        scratch_shapes=[pltpu.SemaphoreType.DMA((6,))],
        compiler_params=pltpu.CompilerParams(vmem_limit_bytes=57 * MB),
        name="pack",
    )(place, ck, cv, sk, sv)


def payload_kernel(own, x, z, zx, q_ref, out_ref):
    lens = [own[0], x[0], z[0], zx[0]]
    out_ref[0:ROWS, :] = q_ref[...]
    q = q_ref[...].astype(F32)
    norm = jnp.max(jnp.sum(q * q, axis=-1, keepdims=True), axis=0, keepdims=True)
    lane = lax.broadcasted_iota(jnp.int32, (16, 128), 1)
    row = jnp.where(lane == 8, norm * 1.02, 0.0)
    for i in range(4):
        row = jnp.where(lane == 2 * i, (lens[i] // 64).astype(F32), row)
        row = jnp.where(lane == 2 * i + 1, (lens[i] % 64).astype(F32), row)
    out_ref[ROWS:ROWS + 16, :] = row.astype(BF16)


def payload(lengths, q):
    smem, vmem = pl.BlockSpec(memory_space=pltpu.SMEM), pl.BlockSpec(memory_space=pltpu.VMEM)
    return pl.pallas_call(
        payload_kernel,
        out_shape=jax.ShapeDtypeStruct((ROWS + 16, HD), BF16),
        in_specs=[smem] * 4 + [vmem],
        out_specs=vmem,
        compiler_params=pltpu.CompilerParams(vmem_limit_bytes=8 * MB),
        name="payload",
    )(*lengths, q)


def assemble_kernel(place, start, *refs):
    qs, bufs, (k_all, v_all, meta, sem) = refs[:4], refs[4:12], refs[12:]
    core, xl, z = place[0], place[1], place[3]
    sign = 1 - 2 * core
    firsts, seconds = bufs[0::2], bufs[1::2]

    def copies(keys, vals):
        pairs = [(k, k_all.at[i]) for i, k in enumerate(keys)] + [(v, v_all.at[i]) for i, v in enumerate(vals)]
        return [pltpu.make_async_copy(s, d, sem.at[i]) for i, (s, d) in enumerate(pairs)]

    def move(keys, vals):
        mine = copies(keys, vals)
        for c in mine:
            c.start()
        for c in mine:
            c.wait()

    pl.when(core == 0)(lambda: move(firsts, seconds))
    pl.when(core == 1)(lambda: move(seconds, firsts))

    lane = lax.broadcasted_iota(jnp.int32, (1, 128), 1)
    rows = [q[ROWS:ROWS + 16, :].astype(F32)[0:1, :] for q in qs]
    pick = lambda i: jnp.where(lane == 2 * i, 64.0, jnp.where(lane == 2 * i + 1, 1.0, 0.0))
    odd = lax.rem(z, 2)
    size = [jnp.sum(rows[0] * pick(i)) for i in range(4)]
    total = functools.reduce(jnp.add, rows)
    before = jnp.zeros((1, 128), F32)
    for j, row in enumerate(rows):
        at = lax.rem(z - 2 * sign * j + 2 * NZ, NZ)
        before += jnp.where(at < z, row, 0.0)
    sums = [jnp.sum(before * pick(i)) for i in range(4)]
    alls = [jnp.sum(total * pick(i)) for i in range(4)]
    low = jnp.where(xl == 0, alls[0] + alls[2], alls[1] + alls[3])
    for i in range(4):
        side, other = i % 2, i // 2
        pairs_before = sums[side] + sums[2 + side]
        own_odd = odd if other == 0 else 1 - odd
        mate = size[(2 - 2 * other) + side]
        offset = pairs_before + jnp.where(own_odd == 1, mate, 0.0)
        upper = xl if side == 0 else 1 - xl
        offset += jnp.where(upper == 1, low, 0.0)
        live = jnp.clip(start[0] - offset.astype(jnp.int32), 0, size[i].astype(jnp.int32))
        meta[i] = live
        zz = z if other == 0 else z + 1 - 2 * odd
        meta[4 + i] = (upper * NZ + zz) * 64
    meta[8] = z
    meta[9] = xl * 512
    meta[10] = sign
    q2 = jnp.sum(jnp.where(lane == 8, functools.reduce(jnp.maximum, rows), 0.0))
    ones = jnp.ones((8, HD), BF16)
    k2 = jnp.zeros((8, 1), F32)
    for i in range(4):
        k = k_all[i]
        norms = lax.dot_general(ones, k * k, (((1,), (1,)), ((), ())), preferred_element_type=F32)
        k2 = jnp.maximum(k2, jnp.max(norms, axis=-1, keepdims=True))
    meta[11] = jnp.where(q2 * jnp.max(k2) * 1.04 <= (SAFE / C2) ** 2, 1, 0).astype(jnp.int32)


def assemble(place, start, qs, bufs):
    smem, vmem = pl.BlockSpec(memory_space=pltpu.SMEM), pl.BlockSpec(memory_space=pltpu.VMEM)
    everything = jax.ShapeDtypeStruct((4,) + bufs[0].shape, BF16)
    return pl.pallas_call(
        assemble_kernel,
        out_shape=[everything, everything, jax.ShapeDtypeStruct((12,), jnp.int32)],
        in_specs=[smem, smem] + [vmem] * 4 + [pl.BlockSpec(memory_space=pl.ANY)] * 8,
        out_specs=[vmem, vmem, smem],
        scratch_shapes=[pltpu.SemaphoreType.DMA((8,))],
        compiler_params=pltpu.CompilerParams(vmem_limit_bytes=24 * MB),
        name="assemble",
    )(place, start, *qs, *bufs)


def unpack_stats(st):
    g = ROWS // 128
    return st[0:g] + st[g:2 * g] + st[2 * g:3 * g], st[3 * g:4 * g] + st[4 * g:5 * g] + st[5 * g:6 * g]


def columns(rows):
    rows = jnp.concatenate([rows, jnp.zeros((128 - rows.shape[0], 128), F32)], axis=0)
    return jnp.transpose(rows)


def attend_kernel(hop, carried, meta, *refs):
    refs = list(refs)
    take = lambda n: [refs.pop(0) for _ in range(n)]
    q_ref, k_all, v_all = take(3)
    came = take(1)[0] if carried else None
    out_ref, meta_out = take(2)
    s_ref, span_ref, m_ref, acc_ref, total_ref = refs
    for i in range(12):
        meta_out[i] = meta[i]
    z, base, sign, small = (meta[i] for i in range(8, 12))
    cache = k_all.shape[1] - 64
    ones = jnp.ones((1024, 128), BF16)
    eye = eye_mask()
    g = ROWS // 128
    token0 = base + lax.rem(z - 2 * sign * hop + 2 * NZ, NZ) * 64

    def scores_of(keys):
        return lax.dot_general(q_ref[0:ROWS, :], keys, (((1,), (1,)), ((), ())), preferred_element_type=F32)

    def span_scores():
        s = scores_of(jnp.concatenate([k_all[i, pl.ds(cache, 64), :] for i in range(4)], axis=0))
        col = lax.broadcasted_iota(jnp.int32, (1, 256), 1)
        owner = col // 64
        pos = col % 64
        for i in range(4):
            pos = jnp.where(owner == i, pos + meta[4 + i], pos)
        row = lax.broadcasted_iota(jnp.int32, s.shape, 0)
        return jnp.where(pos <= token0 + row // 8, s, NEG)

    def span_sums(p):
        values = jnp.concatenate([v_all[i, pl.ds(cache, 64), :] for i in range(4)], axis=0)
        return jnp.dot(p, jnp.concatenate([values, ones[:256]], axis=1), preferred_element_type=F32)

    @pl.when(small == 1)
    def _():
        acc_ref[...] = span_sums(jnp.exp2(span_scores() * C2).astype(BF16))

        def shard(i, carry):
            live = meta[i]

            def piece(first, size):
                at = pl.ds(pl.multiple_of(first, 256), size)
                slot = first + lax.broadcasted_iota(jnp.int32, (1, size), 1)
                bias = jnp.where(slot < live, 0.0, NEG)
                p = jnp.exp2(scores_of(k_all[i, at, :]) * C2 + bias).astype(BF16)
                v = jnp.concatenate([v_all[i, at, :], ones[:size]], axis=1)
                acc_ref[...] += jnp.dot(p, v, preferred_element_type=F32)

            def body(t, carry):
                piece(t * 1024, 1024)
                return carry

            n = (live + 255) // 256
            whole = n // 4
            lax.fori_loop(0, whole, body, 0)
            pl.when(n % 4 >= 2)(lambda: piece(whole * 1024, 512))
            pl.when(n % 2 == 1)(lambda: piece((n - 1) * 256, 256))
            return carry

        lax.fori_loop(0, 4, shard, 0)
        m_ref[...] = jnp.where(acc_ref[:, 128:256] > 0.0, 0.0, NEG)

    @pl.when(small == 0)
    def _():
        half = lambda x: functools.reduce(jnp.maximum, [x[:, j:j + 128] for j in range(0, x.shape[1], 128)])
        s = span_scores()
        span_ref[...] = s
        m_ref[...] = half(s)

        def score_shard(i, first):
            live = meta[i]
            tiles = (live + TILE - 1) // TILE

            def score(t, carry):
                at = pl.ds(pl.multiple_of(t * TILE, TILE), TILE)
                slot = t * TILE + lax.broadcasted_iota(jnp.int32, (1, TILE), 1)
                s = scores_of(k_all[i, at, :]) + jnp.where(slot < live, 0.0, NEG)
                s_ref[first + t] = s
                m_ref[...] = jnp.maximum(m_ref[...], half(s))
                return carry

            lax.fori_loop(0, tiles, score, 0)
            return first + tiles

        lax.fori_loop(0, 4, score_shard, jnp.int32(0))
        m = jnp.broadcast_to(jnp.max(m_ref[...], axis=-1, keepdims=True), (ROWS, 128))
        m_ref[...] = m
        s = span_ref[...]
        wide = jnp.concatenate([m, m], axis=1)
        acc_ref[...] = span_sums(jnp.where(s > 0.5 * NEG, jnp.exp2((s - wide) * C2), 0.0).astype(BF16))

        def value_shard(i, first):
            tiles = (meta[i] + TILE - 1) // TILE

            def value(t, carry):
                at = pl.ds(pl.multiple_of(t * TILE, TILE), TILE)
                wide = jnp.concatenate([m_ref[...]] * (TILE // 128), axis=1)
                p = jnp.exp2((s_ref[first + t] - wide) * C2).astype(BF16)
                v = jnp.concatenate([v_all[i, at, :], ones[:TILE]], axis=1)
                acc_ref[...] += jnp.dot(p, v, preferred_element_type=F32)
                return carry

            lax.fori_loop(0, tiles, value, 0)
            return first + tiles

        lax.fori_loop(0, 4, value_shard, jnp.int32(0))

    if carried:
        ms, ls = unpack_stats(came[ROWS:ROWS + STAT, :].astype(F32))
        ft = columns(jnp.concatenate([ms, ls], axis=0))
        for r in range(g):
            at = slice(r * 128, (r + 1) * 128)
            m_in = jnp.broadcast_to(ft[:, r:r + 1], (128, 128))
            l_in = jnp.broadcast_to(ft[:, g + r:g + r + 1], (128, 128))
            m_own = m_ref[at, :]
            m = jnp.maximum(m_own, m_in)
            w_own = jnp.exp2((m_own - m) * C2)
            w_in = jnp.exp2((m_in - m) * C2) * l_in
            total = acc_ref[at, 128:256] * w_own + w_in
            mixed = acc_ref[at, 0:128] * w_own + came[at, :].astype(F32) * w_in
            out_ref[at, :] = (mixed / jnp.maximum(total, 1e-35)).astype(BF16)
            m_ref[at, :] = m
            total_ref[at, :] = total
    else:
        total = acc_ref[:, 128:256]
        out_ref[0:ROWS, :] = (acc_ref[:, 0:128] / jnp.maximum(total, 1e-35)).astype(BF16)
        total_ref[...] = total

    compact = lambda x: jnp.sum(jnp.where(eye[None], x.reshape(g, 128, 128), 0.0), axis=1)
    stats = split3(compact(m_ref[...])) + split3(compact(total_ref[...]))
    pad = jnp.zeros((STAT - 6 * g, 128), F32)
    out_ref[ROWS:ROWS + STAT, :] = jnp.concatenate([x.astype(F32) for x in stats] + [pad], axis=0).astype(BF16)


def attend(hop, meta, q, k_all, v_all, came):
    smem, vmem = pl.BlockSpec(memory_space=pltpu.SMEM), pl.BlockSpec(memory_space=pltpu.VMEM)
    tiles = 4 * (k_all.shape[1] - 64) // TILE
    came = [] if came is None else [came]
    return pl.pallas_call(
        functools.partial(attend_kernel, hop, bool(came)),
        out_shape=[jax.ShapeDtypeStruct((ROWS + STAT, 128), BF16), jax.ShapeDtypeStruct((12,), jnp.int32)],
        in_specs=[smem] + [vmem] * (3 + len(came)),
        out_specs=[vmem, smem],
        scratch_shapes=[
            pltpu.VMEM((tiles, ROWS, TILE), F32),
            pltpu.VMEM((ROWS, 256), F32),
            pltpu.VMEM((ROWS, 128), F32),
            pltpu.VMEM((ROWS, 256), F32),
            pltpu.VMEM((ROWS, 128), F32),
        ],
        compiler_params=pltpu.CompilerParams(vmem_limit_bytes=28 * MB),
        cost_estimate=pl.CostEstimate(flops=600_000_000, bytes_accessed=100_000, transcendentals=1_000),
        name="attend",
    )(meta, q, k_all, v_all, *came)


def combine_kernel(place, *refs):
    parts, (out_ref, *piece_refs, f_ref, flat_ref) = refs[:-7], refs[-7:]
    g = ROWS // 128
    ms, ls = zip(*[unpack_stats(ref[ROWS:ROWS + STAT, :].astype(F32)) for ref in parts])
    top = functools.reduce(jnp.maximum, ms)
    ws = [jnp.exp2((m - top) * C2) * l for m, l in zip(ms, ls)]
    whole = functools.reduce(jnp.add, ws)
    ft = columns(jnp.concatenate([w / whole for w in ws], axis=0))
    for r in range(g):
        total = jnp.zeros((128, 128), F32)
        for k, ref in enumerate(parts):
            total += ref[r * 128:(r + 1) * 128, :].astype(F32) * ft[:, k * g + r:k * g + r + 1]
        out_ref[r * 128:(r + 1) * 128, :] = total.astype(BF16)
        f_ref[r * 128:(r + 1) * 128, :] = total
    for h in range(8):
        flat_ref[:, h * 128:(h + 1) * 128] = f_ref[pl.ds(h, 64, stride=8), :].astype(BF16)
    core, xl = place[0], place[1]
    for i, ref in enumerate(piece_refs):
        c = core if i % 2 == 0 else 1 - core
        x = xl if i // 2 == 0 else 1 - xl
        ref[...] = flat_ref[pl.ds(pl.multiple_of(x * 32 + c * 16, 16), 16), :]


def combine(place, parts):
    vmem = pl.BlockSpec(memory_space=pltpu.VMEM)
    piece = jax.ShapeDtypeStruct((16, 1024), BF16)
    return pl.pallas_call(
        combine_kernel,
        out_shape=[jax.ShapeDtypeStruct((ROWS, 128), BF16)] + [piece] * 4,
        in_specs=[pl.BlockSpec(memory_space=pltpu.SMEM)] + [vmem] * len(parts),
        out_specs=[vmem] * 5,
        scratch_shapes=[pltpu.VMEM((ROWS, 128), F32), pltpu.VMEM((64, 1024), BF16)],
        compiler_params=pltpu.CompilerParams(vmem_limit_bytes=16 * MB),
        name="combine",
    )(place, *parts)


def local(queries, cache_keys, cache_values, span_keys, span_values, span_start, cache_lengths, out_weight):
    xl, z, y, xh, core = (lax.axis_index(a) for a in ("xl", "z", "y", "xh", "core"))
    sign = 1 - 2 * core
    kv = y * 2 + xh
    place = jnp.stack([core, xl, kv, z]).astype(jnp.int32)

    def shift(x, k):
        pairs = [(b * 2 + c, (b + k * (1 - 2 * c)) % NZ * 2 + c) for b in range(NZ) for c in range(2)]
        return lax.ppermute(x, ("z", "core"), pairs)

    swap = [(0, 1), (1, 0)]
    cross = [(i, 3 - i) for i in range(4)]
    mate = [(i, i ^ 1) for i in range(NZ)]

    near, far, rest = pack(place, cache_keys, cache_values, span_keys, span_values)
    got_x = lax.ppermute(far, ("xl", "xh"), cross)
    got_z = lax.ppermute(near, "z", mate)

    both = [((a * NZ + b) * 2 + c, ((1 - a) * NZ + (b ^ 1)) * 2 + 1 - c) for a in range(2) for b in range(NZ) for c in range(2)]
    lengths = [
        cache_lengths,
        lax.ppermute(cache_lengths, ("xl", "xh"), cross),
        lax.ppermute(cache_lengths, "z", mate),
        lax.ppermute(cache_lengths, ("xl", "z", "xh"), both),
    ]
    q = payload(lengths, queries.reshape(ROWS, HD))
    q_blocks = [q, shift(q, 2), None, shift(q, -2)]
    q_blocks[2] = shift(q_blocks[1], 2)
    got_x, got_z, q_blocks[2], q_blocks[3], weight = lax.optimization_barrier(
        (got_x, got_z, q_blocks[2], q_blocks[3], out_weight)
    )
    got_zx = lax.ppermute(got_x, "z", mate)
    w_x = lax.ppermute(weight, "xl", swap)
    w_core = lax.ppermute(weight, "core", swap)
    bufs = [near, rest]
    for got in (got_x, got_z, got_zx):
        bufs += [got, lax.ppermute(got, "core", swap)]
    k_all, v_all, meta = assemble(place, span_start, q_blocks, bufs)

    out, meta = attend(2, meta, q_blocks[2], k_all, v_all, None)
    half_way = shift(out, 2)
    out, meta = attend(1, meta, q_blocks[1], k_all, v_all, None)
    down = shift(out, -2)
    out, meta = attend(3, meta, q_blocks[3], k_all, v_all, half_way)
    up = shift(out, 2)
    own, meta = attend(0, meta, q_blocks[0], k_all, v_all, None)
    own, w_x = lax.optimization_barrier((own, w_x))
    w_both = lax.ppermute(w_x, "core", swap)
    mixed, *pieces = combine(place, [own, up, down])
    attended = mixed.reshape(64, 8, HD)

    p_core = lax.ppermute(pieces[1], "core", swap)
    p_x = lax.ppermute(pieces[2], "xl", swap)
    p_both = lax.ppermute(pieces[3], ("xl", "core"), cross)
    here = jnp.concatenate([pieces[0], p_core], axis=1)
    there = jnp.concatenate([p_x, p_both], axis=1)
    pair = jnp.stack([jnp.where(xl == 0, here, there), jnp.where(xl == 0, there, here)])[:, None]
    every = jnp.zeros((2, NZ, 16, 2048), BF16)
    every = lax.dynamic_update_slice(every, pair, (0, z, 0, 0))
    up = down = pair
    for k in range(1, 5):
        up = shift(up, 1)
        every = lax.dynamic_update_slice(every, up, (0, (z - sign * k + 2 * NZ) % NZ, 0, 0))
        if k < 4:
            down = shift(down, -1)
            every = lax.dynamic_update_slice(every, down, (0, (z + sign * k + 2 * NZ) % NZ, 0, 0))
    x = every.reshape(256, 2048)

    def term(top, low):
        part = jnp.dot(x[:, 0:1024], top, preferred_element_type=F32)
        return (part + jnp.dot(x[:, 1024:2048], low, preferred_element_type=F32)).astype(BF16)

    t_own, t_peer = term(out_weight, w_core), term(w_x, w_both)
    terms = jnp.stack([jnp.where(xl == 0, t_own, t_peer), jnp.where(xl == 0, t_peer, t_own)])
    got = lax.all_to_all(terms.reshape(32, 16, 1024), ("xl", "y", "xh", "core"), 0, 0, tiled=True)
    projected = jnp.sum(got.reshape(2, 8, 2, 16, 1024).astype(F32), axis=1).astype(BF16).reshape(64, 1024)
    return attended, projected


def solution(mesh):
    fine = Mesh(mesh.devices.reshape(2, NZ, 4, 2, 2), ("xl", "z", "y", "xh", "core"))
    ctx, tp = ("xl", "z"), ("y", "xh", "core")
    return jax.shard_map(
        local,
        mesh=fine,
        in_specs=(
            P(ctx, tp, None),
            P(None, ctx, None),
            P(None, ctx, None),
            P(None, ctx, None),
            P(None, ctx, None),
            P(),
            P(ctx),
            P(tp, ctx),
        ),
        out_specs=(P(ctx, tp, None), P(tp, ctx)),
        check_vma=False,
    )
```

```python
import functools
import math

import jax
import jax.numpy as jnp
from jax import lax
from jax.experimental import pallas as pl
from jax.experimental.pallas import tpu as pltpu
from jax.sharding import Mesh, PartitionSpec as P

H = 128
KVH = 8
HD = 128
NEG = -1e30
SCALE = 1.0 / math.sqrt(HD)
C2 = math.log2(math.e) * SCALE
TILE = 512
ROWS = 512
STAT = 32
NZ = 8
SAFE = 90.0
F32 = jnp.float32
BF16 = jnp.bfloat16
MB = 1024 * 1024


def eye_mask():
    r = lax.broadcasted_iota(jnp.int32, (128, 128), 0)
    c = lax.broadcasted_iota(jnp.int32, (128, 128), 1)
    return r == c


def split3(x):
    hi = x.astype(BF16)
    rest = x - hi.astype(F32)
    mid = rest.astype(BF16)
    lo = (rest - mid.astype(F32)).astype(BF16)
    return hi, mid, lo


def pack_kernel(place, ck, cv, sk, sv, near_out, far_out, rest_out, sem):
    core, kv = place[0], place[2]
    n = ck.shape[1]

    def copies(cache, span, out, head, first):
        return [
            pltpu.make_async_copy(cache.at[head], out.at[pl.ds(0, n)], sem.at[first]),
            pltpu.make_async_copy(span.at[head], out.at[pl.ds(n, 64)], sem.at[first + 1]),
        ]

    def move(cache, span, cache2, span2):
        mine = copies(cache, span, far_out, kv ^ 1, 0) + copies(cache, span, near_out, kv, 2)
        mine += copies(cache2, span2, rest_out, kv, 4)
        for c in mine:
            c.start()
        for c in mine:
            c.wait()

    pl.when(core == 0)(lambda: move(ck, sk, cv, sv))
    pl.when(core == 1)(lambda: move(cv, sv, ck, sk))


def pack(place, ck, cv, sk, sv):
    n = ck.shape[1] + 64
    shape = jax.ShapeDtypeStruct((n, HD), BF16)
    return pl.pallas_call(
        pack_kernel,
        out_shape=[shape] * 3,
        in_specs=[pl.BlockSpec(memory_space=pltpu.SMEM)] + [pl.BlockSpec(memory_space=pl.ANY)] * 4,
        out_specs=[pl.BlockSpec(memory_space=pltpu.VMEM)] * 3,
        scratch_shapes=[pltpu.SemaphoreType.DMA((6,))],
        compiler_params=pltpu.CompilerParams(vmem_limit_bytes=57 * MB),
        name="pack",
    )(place, ck, cv, sk, sv)


def payload_kernel(own, x, z, zx, q_ref, out_ref):
    lens = [own[0], x[0], z[0], zx[0]]
    out_ref[0:ROWS, :] = q_ref[...]
    q = q_ref[...].astype(F32)
    norm = jnp.max(jnp.sum(q * q, axis=-1, keepdims=True), axis=0, keepdims=True)
    lane = lax.broadcasted_iota(jnp.int32, (16, 128), 1)
    row = jnp.where(lane == 8, norm * 1.02, 0.0)
    for i in range(4):
        row = jnp.where(lane == 2 * i, (lens[i] // 64).astype(F32), row)
        row = jnp.where(lane == 2 * i + 1, (lens[i] % 64).astype(F32), row)
    out_ref[ROWS:ROWS + 16, :] = row.astype(BF16)


def payload(lengths, q):
    smem, vmem = pl.BlockSpec(memory_space=pltpu.SMEM), pl.BlockSpec(memory_space=pltpu.VMEM)
    return pl.pallas_call(
        payload_kernel,
        out_shape=jax.ShapeDtypeStruct((ROWS + 16, HD), BF16),
        in_specs=[smem] * 4 + [vmem],
        out_specs=vmem,
        compiler_params=pltpu.CompilerParams(vmem_limit_bytes=8 * MB),
        name="payload",
    )(*lengths, q)


def assemble_kernel(place, start, *refs):
    qs, bufs, (k_all, v_all, meta, sem) = refs[:4], refs[4:12], refs[12:]
    core, xl, z = place[0], place[1], place[3]
    sign = 1 - 2 * core
    firsts, seconds = bufs[0::2], bufs[1::2]

    def copies(keys, vals):
        pairs = [(k, k_all.at[i]) for i, k in enumerate(keys)] + [(v, v_all.at[i]) for i, v in enumerate(vals)]
        return [pltpu.make_async_copy(s, d, sem.at[i]) for i, (s, d) in enumerate(pairs)]

    def move(keys, vals):
        mine = copies(keys, vals)
        for c in mine:
            c.start()
        for c in mine:
            c.wait()

    pl.when(core == 0)(lambda: move(firsts, seconds))
    pl.when(core == 1)(lambda: move(seconds, firsts))

    lane = lax.broadcasted_iota(jnp.int32, (1, 128), 1)
    rows = [q[ROWS:ROWS + 16, :].astype(F32)[0:1, :] for q in qs]
    pick = lambda i: jnp.where(lane == 2 * i, 64.0, jnp.where(lane == 2 * i + 1, 1.0, 0.0))
    odd = lax.rem(z, 2)
    size = [jnp.sum(rows[0] * pick(i)) for i in range(4)]
    total = functools.reduce(jnp.add, rows)
    before = jnp.zeros((1, 128), F32)
    for j, row in enumerate(rows):
        at = lax.rem(z - 2 * sign * j + 2 * NZ, NZ)
        before += jnp.where(at < z, row, 0.0)
    sums = [jnp.sum(before * pick(i)) for i in range(4)]
    alls = [jnp.sum(total * pick(i)) for i in range(4)]
    low = jnp.where(xl == 0, alls[0] + alls[2], alls[1] + alls[3])
    for i in range(4):
        side, other = i % 2, i // 2
        pairs_before = sums[side] + sums[2 + side]
        own_odd = odd if other == 0 else 1 - odd
        mate = size[(2 - 2 * other) + side]
        offset = pairs_before + jnp.where(own_odd == 1, mate, 0.0)
        upper = xl if side == 0 else 1 - xl
        offset += jnp.where(upper == 1, low, 0.0)
        live = jnp.clip(start[0] - offset.astype(jnp.int32), 0, size[i].astype(jnp.int32))
        meta[i] = live
        zz = z if other == 0 else z + 1 - 2 * odd
        meta[4 + i] = (upper * NZ + zz) * 64
    meta[8] = z
    meta[9] = xl * 512
    meta[10] = sign
    q2 = jnp.sum(jnp.where(lane == 8, functools.reduce(jnp.maximum, rows), 0.0))
    ones = jnp.ones((8, HD), BF16)
    k2 = jnp.zeros((8, 1), F32)
    for i in range(4):
        k = k_all[i]
        norms = lax.dot_general(ones, k * k, (((1,), (1,)), ((), ())), preferred_element_type=F32)
        k2 = jnp.maximum(k2, jnp.max(norms, axis=-1, keepdims=True))
    meta[11] = jnp.where(q2 * jnp.max(k2) * 1.04 <= (SAFE / C2) ** 2, 1, 0).astype(jnp.int32)


def assemble(place, start, qs, bufs):
    smem, vmem = pl.BlockSpec(memory_space=pltpu.SMEM), pl.BlockSpec(memory_space=pltpu.VMEM)
    everything = jax.ShapeDtypeStruct((4,) + bufs[0].shape, BF16)
    return pl.pallas_call(
        assemble_kernel,
        out_shape=[everything, everything, jax.ShapeDtypeStruct((12,), jnp.int32)],
        in_specs=[smem, smem] + [vmem] * 4 + [pl.BlockSpec(memory_space=pl.ANY)] * 8,
        out_specs=[vmem, vmem, smem],
        scratch_shapes=[pltpu.SemaphoreType.DMA((8,))],
        compiler_params=pltpu.CompilerParams(vmem_limit_bytes=24 * MB),
        name="assemble",
    )(place, start, *qs, *bufs)


def unpack_stats(st):
    g = ROWS // 128
    return st[0:g] + st[g:2 * g] + st[2 * g:3 * g], st[3 * g:4 * g] + st[4 * g:5 * g] + st[5 * g:6 * g]


def columns(rows):
    rows = jnp.concatenate([rows, jnp.zeros((128 - rows.shape[0], 128), F32)], axis=0)
    return jnp.transpose(rows)


def attend_kernel(hop, carried, meta, *refs):
    refs = list(refs)
    take = lambda n: [refs.pop(0) for _ in range(n)]
    q_ref, k_all, v_all = take(3)
    came = take(1)[0] if carried else None
    out_ref, meta_out = take(2)
    s_ref, span_ref, m_ref, acc_ref, total_ref = refs
    for i in range(12):
        meta_out[i] = meta[i]
    z, base, sign, small = (meta[i] for i in range(8, 12))
    cache = k_all.shape[1] - 64
    ones = jnp.ones((1024, 128), BF16)
    eye = eye_mask()
    g = ROWS // 128
    token0 = base + lax.rem(z - 2 * sign * hop + 2 * NZ, NZ) * 64

    def scores_of(keys):
        return lax.dot_general(q_ref[0:ROWS, :], keys, (((1,), (1,)), ((), ())), preferred_element_type=F32)

    def span_scores():
        s = scores_of(jnp.concatenate([k_all[i, pl.ds(cache, 64), :] for i in range(4)], axis=0))
        col = lax.broadcasted_iota(jnp.int32, (1, 256), 1)
        owner = col // 64
        pos = col % 64
        for i in range(4):
            pos = jnp.where(owner == i, pos + meta[4 + i], pos)
        row = lax.broadcasted_iota(jnp.int32, s.shape, 0)
        return jnp.where(pos <= token0 + row // 8, s, NEG)

    def span_sums(p):
        values = jnp.concatenate([v_all[i, pl.ds(cache, 64), :] for i in range(4)], axis=0)
        return jnp.dot(p, jnp.concatenate([values, ones[:256]], axis=1), preferred_element_type=F32)

    @pl.when(small == 1)
    def _():
        acc_ref[...] = span_sums(jnp.exp(span_scores() * SCALE).astype(BF16))

        def shard(i, carry):
            live = meta[i]

            def piece(first, size, masked):
                def scores(j):
                    at = pl.ds(pl.multiple_of(first + j * 256, 256), 256)
                    return scores_of(k_all[i, at, :])

                total = acc_ref[...]
                ahead = scores(0)
                for j in range(size // 256):
                    s = ahead * SCALE
                    if j + 1 < size // 256:
                        ahead = scores(j + 1)
                    if masked:
                        slot = first + j * 256 + lax.broadcasted_iota(jnp.int32, (1, 256), 1)
                        s = s + jnp.where(slot < live, 0.0, NEG)
                    p = jnp.exp(s).astype(BF16)
                    at = pl.ds(pl.multiple_of(first + j * 256, 256), 256)
                    v = jnp.concatenate([v_all[i, at, :], ones[:256]], axis=1)
                    total = total + jnp.dot(p, v, preferred_element_type=F32)
                acc_ref[...] = total

            def body(t, carry):
                piece(t * 1024, 1024, False)
                return carry

            whole = live // 1024
            first = whole * 1024
            n = (live - first + 255) // 256
            lax.fori_loop(0, whole, body, 0)
            pl.when(n == 4)(lambda: piece(first, 1024, True))
            pl.when((n == 2) | (n == 3))(lambda: piece(first, 512, True))
            pl.when((n == 1) | (n == 3))(lambda: piece(first + (n - 1) * 256, 256, True))
            return carry

        lax.fori_loop(0, 4, shard, 0)
        m_ref[...] = jnp.where(acc_ref[:, 128:256] > 0.0, 0.0, NEG)

    @pl.when(small == 0)
    def _():
        half = lambda x: functools.reduce(jnp.maximum, [x[:, j:j + 128] for j in range(0, x.shape[1], 128)])
        s = span_scores()
        span_ref[...] = s
        m_ref[...] = half(s)

        def score_shard(i, first):
            live = meta[i]
            tiles = (live + TILE - 1) // TILE

            def score(t, carry):
                at = pl.ds(pl.multiple_of(t * TILE, TILE), TILE)
                slot = t * TILE + lax.broadcasted_iota(jnp.int32, (1, TILE), 1)
                s = scores_of(k_all[i, at, :]) + jnp.where(slot < live, 0.0, NEG)
                s_ref[first + t] = s
                m_ref[...] = jnp.maximum(m_ref[...], half(s))
                return carry

            lax.fori_loop(0, tiles, score, 0)
            return first + tiles

        lax.fori_loop(0, 4, score_shard, jnp.int32(0))
        m = jnp.broadcast_to(jnp.max(m_ref[...], axis=-1, keepdims=True), (ROWS, 128))
        m_ref[...] = m
        s = span_ref[...]
        wide = jnp.concatenate([m, m], axis=1)
        acc_ref[...] = span_sums(jnp.where(s > 0.5 * NEG, jnp.exp2((s - wide) * C2), 0.0).astype(BF16))

        def value_shard(i, first):
            tiles = (meta[i] + TILE - 1) // TILE

            def value(t, carry):
                at = pl.ds(pl.multiple_of(t * TILE, TILE), TILE)
                wide = jnp.concatenate([m_ref[...]] * (TILE // 128), axis=1)
                p = jnp.exp2((s_ref[first + t] - wide) * C2).astype(BF16)
                v = jnp.concatenate([v_all[i, at, :], ones[:TILE]], axis=1)
                acc_ref[...] += jnp.dot(p, v, preferred_element_type=F32)
                return carry

            lax.fori_loop(0, tiles, value, 0)
            return first + tiles

        lax.fori_loop(0, 4, value_shard, jnp.int32(0))

    if carried:
        ms, ls = unpack_stats(came[ROWS:ROWS + STAT, :].astype(F32))
        ft = columns(jnp.concatenate([ms, ls], axis=0))
        for r in range(g):
            at = slice(r * 128, (r + 1) * 128)
            m_in = jnp.broadcast_to(ft[:, r:r + 1], (128, 128))
            l_in = jnp.broadcast_to(ft[:, g + r:g + r + 1], (128, 128))
            m_own = m_ref[at, :]
            m = jnp.maximum(m_own, m_in)
            w_own = jnp.exp2((m_own - m) * C2)
            w_in = jnp.exp2((m_in - m) * C2) * l_in
            total = acc_ref[at, 128:256] * w_own + w_in
            mixed = acc_ref[at, 0:128] * w_own + came[at, :].astype(F32) * w_in
            out_ref[at, :] = (mixed / jnp.maximum(total, 1e-35)).astype(BF16)
            m_ref[at, :] = m
            total_ref[at, :] = total
    else:
        total = acc_ref[:, 128:256]
        out_ref[0:ROWS, :] = (acc_ref[:, 0:128] / jnp.maximum(total, 1e-35)).astype(BF16)
        total_ref[...] = total

    compact = lambda x: jnp.sum(jnp.where(eye[None], x.reshape(g, 128, 128), 0.0), axis=1)
    stats = split3(compact(m_ref[...])) + split3(compact(total_ref[...]))
    pad = jnp.zeros((STAT - 6 * g, 128), F32)
    out_ref[ROWS:ROWS + STAT, :] = jnp.concatenate([x.astype(F32) for x in stats] + [pad], axis=0).astype(BF16)


def attend(hop, meta, q, k_all, v_all, came):
    smem, vmem = pl.BlockSpec(memory_space=pltpu.SMEM), pl.BlockSpec(memory_space=pltpu.VMEM)
    tiles = 4 * (k_all.shape[1] - 64) // TILE
    came = [] if came is None else [came]
    return pl.pallas_call(
        functools.partial(attend_kernel, hop, bool(came)),
        out_shape=[jax.ShapeDtypeStruct((ROWS + STAT, 128), BF16), jax.ShapeDtypeStruct((12,), jnp.int32)],
        in_specs=[smem] + [vmem] * (3 + len(came)),
        out_specs=[vmem, smem],
        scratch_shapes=[
            pltpu.VMEM((tiles, ROWS, TILE), F32),
            pltpu.VMEM((ROWS, 256), F32),
            pltpu.VMEM((ROWS, 128), F32),
            pltpu.VMEM((ROWS, 256), F32),
            pltpu.VMEM((ROWS, 128), F32),
        ],
        compiler_params=pltpu.CompilerParams(vmem_limit_bytes=28 * MB),
        cost_estimate=pl.CostEstimate(flops=600_000_000, bytes_accessed=100_000, transcendentals=1_000),
        name="attend",
    )(meta, q, k_all, v_all, *came)


def combine_kernel(place, *refs):
    parts, (out_ref, *piece_refs, f_ref, flat_ref) = refs[:-7], refs[-7:]
    g = ROWS // 128
    ms, ls = zip(*[unpack_stats(ref[ROWS:ROWS + STAT, :].astype(F32)) for ref in parts])
    top = functools.reduce(jnp.maximum, ms)
    ws = [jnp.exp2((m - top) * C2) * l for m, l in zip(ms, ls)]
    whole = functools.reduce(jnp.add, ws)
    ft = columns(jnp.concatenate([w / whole for w in ws], axis=0))
    for r in range(g):
        total = jnp.zeros((128, 128), F32)
        for k, ref in enumerate(parts):
            total += ref[r * 128:(r + 1) * 128, :].astype(F32) * ft[:, k * g + r:k * g + r + 1]
        out_ref[r * 128:(r + 1) * 128, :] = total.astype(BF16)
        f_ref[r * 128:(r + 1) * 128, :] = total
    for h in range(8):
        flat_ref[:, h * 128:(h + 1) * 128] = f_ref[pl.ds(h, 64, stride=8), :].astype(BF16)
    core, xl = place[0], place[1]
    for i, ref in enumerate(piece_refs):
        c = core if i % 2 == 0 else 1 - core
        x = xl if i // 2 == 0 else 1 - xl
        ref[...] = flat_ref[pl.ds(pl.multiple_of(x * 32 + c * 16, 16), 16), :]


def combine(place, parts):
    vmem = pl.BlockSpec(memory_space=pltpu.VMEM)
    piece = jax.ShapeDtypeStruct((16, 1024), BF16)
    return pl.pallas_call(
        combine_kernel,
        out_shape=[jax.ShapeDtypeStruct((ROWS, 128), BF16)] + [piece] * 4,
        in_specs=[pl.BlockSpec(memory_space=pltpu.SMEM)] + [vmem] * len(parts),
        out_specs=[vmem] * 5,
        scratch_shapes=[pltpu.VMEM((ROWS, 128), F32), pltpu.VMEM((64, 1024), BF16)],
        compiler_params=pltpu.CompilerParams(vmem_limit_bytes=16 * MB),
        name="combine",
    )(place, *parts)


def local(queries, cache_keys, cache_values, span_keys, span_values, span_start, cache_lengths, out_weight):
    xl, z, y, xh, core = (lax.axis_index(a) for a in ("xl", "z", "y", "xh", "core"))
    sign = 1 - 2 * core
    kv = y * 2 + xh
    place = jnp.stack([core, xl, kv, z]).astype(jnp.int32)

    def shift(x, k):
        pairs = [(b * 2 + c, (b + k * (1 - 2 * c)) % NZ * 2 + c) for b in range(NZ) for c in range(2)]
        return lax.ppermute(x, ("z", "core"), pairs)

    swap = [(0, 1), (1, 0)]
    cross = [(i, 3 - i) for i in range(4)]
    mate = [(i, i ^ 1) for i in range(NZ)]

    both = [((a * NZ + b) * 2 + c, ((1 - a) * NZ + (b ^ 1)) * 2 + 1 - c) for a in range(2) for b in range(NZ) for c in range(2)]
    lengths = [
        cache_lengths,
        lax.ppermute(cache_lengths, ("xl", "xh"), cross),
        lax.ppermute(cache_lengths, "z", mate),
        lax.ppermute(cache_lengths, ("xl", "z", "xh"), both),
    ]

    near, far, rest = pack(place, cache_keys, cache_values, span_keys, span_values)
    near, far, lengths = lax.optimization_barrier((near, far, lengths))
    got_x = lax.ppermute(far, ("xl", "xh"), cross)
    got_z = lax.ppermute(near, "z", mate)

    q = payload(lengths, queries.reshape(ROWS, HD))
    q_blocks = [q, shift(q, 2), None, shift(q, -2)]
    got_z, q_blocks[1], q_blocks[3] = lax.optimization_barrier((got_z, q_blocks[1], q_blocks[3]))
    q_blocks[2] = shift(q_blocks[1], 2)
    got_zx = lax.ppermute(got_z, "xl", swap)
    got_x, got_z, got_zx, q_blocks[2], q_blocks[3], weight = lax.optimization_barrier(
        (got_x, got_z, got_zx, q_blocks[2], q_blocks[3], out_weight)
    )
    w_x1 = lax.ppermute(weight[0:512], "xl", swap)
    bufs = [near, rest]
    for got in (got_x, got_z, got_zx):
        bufs += [got, lax.ppermute(got, "core", swap)]
    k_all, v_all, meta = assemble(place, span_start, q_blocks, bufs)

    out, meta = attend(2, meta, q_blocks[2], k_all, v_all, None)
    half_way = shift(out, 2)
    out, meta = attend(1, meta, q_blocks[1], k_all, v_all, None)
    down = shift(out, -2)
    out, meta = attend(3, meta, q_blocks[3], k_all, v_all, half_way)
    up = shift(out, 2)
    own, meta = attend(0, meta, q_blocks[0], k_all, v_all, None)
    own, w_x1 = lax.optimization_barrier((own, w_x1))
    mixed, *pieces = combine(place, [own, up, down])
    attended = mixed.reshape(64, 8, HD)

    p_core = lax.ppermute(pieces[1], "core", swap)
    p_x = lax.ppermute(pieces[2], "xl", swap)
    p_both = lax.ppermute(pieces[3], ("xl", "core"), cross)
    p_core, p_x, p_both, weight = lax.optimization_barrier((p_core, p_x, p_both, weight))
    w_x2 = lax.ppermute(weight[512:1024], "xl", swap)
    w_core = lax.ppermute(weight, "core", swap)
    w_both1 = lax.ppermute(w_x1, "core", swap)
    w_both2 = lax.ppermute(w_x2, "core", swap)
    here = jnp.concatenate([pieces[0], p_core], axis=1)
    there = jnp.concatenate([p_x, p_both], axis=1)
    pair = jnp.stack([jnp.where(xl == 0, here, there), jnp.where(xl == 0, there, here)])[:, None]
    every = jnp.zeros((2, NZ, 16, 2048), BF16)
    every = lax.dynamic_update_slice(every, pair, (0, z, 0, 0))
    up = down = pair
    for k in range(1, 5):
        up = shift(up, 1)
        every = lax.dynamic_update_slice(every, up, (0, (z - sign * k + 2 * NZ) % NZ, 0, 0))
        if k < 4:
            down = shift(down, -1)
            every = lax.dynamic_update_slice(every, down, (0, (z + sign * k + 2 * NZ) % NZ, 0, 0))
    x = every.reshape(256, 2048)

    def term(*blocks):
        total, at = 0.0, 0
        for w in blocks:
            total = total + jnp.dot(x[:, at:at + w.shape[0]], w, preferred_element_type=F32)
            at += w.shape[0]
        return total.astype(BF16)

    t_own, t_peer = term(out_weight, w_core), term(w_x1, w_x2, w_both1, w_both2)
    terms = jnp.stack([jnp.where(xl == 0, t_own, t_peer), jnp.where(xl == 0, t_peer, t_own)])
    got = lax.all_to_all(terms.reshape(32, 16, 1024), ("xl", "y", "xh", "core"), 0, 0, tiled=True)
    projected = jnp.sum(got.reshape(2, 8, 2, 16, 1024).astype(F32), axis=1).astype(BF16).reshape(64, 1024)
    return attended, projected


def solution(mesh):
    fine = Mesh(mesh.devices.reshape(2, NZ, 4, 2, 2), ("xl", "z", "y", "xh", "core"))
    ctx, tp = ("xl", "z"), ("y", "xh", "core")
    return jax.shard_map(
        local,
        mesh=fine,
        in_specs=(
            P(ctx, tp, None),
            P(None, ctx, None),
            P(None, ctx, None),
            P(None, ctx, None),
            P(None, ctx, None),
            P(),
            P(ctx),
            P(tp, ctx),
        ),
        out_specs=(P(ctx, tp, None), P(tp, ctx)),
        check_vma=False,
    )
```

```python
import functools
import math

import jax
import jax.numpy as jnp
from jax import lax
from jax.experimental import pallas as pl
from jax.experimental.pallas import tpu as pltpu
from jax.sharding import Mesh, PartitionSpec as P

H = 128
KVH = 8
HD = 128
NEG = -1e30
SCALE = 1.0 / math.sqrt(HD)
C2 = math.log2(math.e) * SCALE
TILE = 256
ROWS = 512
STAT = 32
NZ = 8
SAFE = 90.0
F32 = jnp.float32
BF16 = jnp.bfloat16
MB = 1024 * 1024


def eye_mask():
    r = lax.broadcasted_iota(jnp.int32, (128, 128), 0)
    c = lax.broadcasted_iota(jnp.int32, (128, 128), 1)
    return r == c


def split3(x):
    hi = x.astype(BF16)
    rest = x - hi.astype(F32)
    mid = rest.astype(BF16)
    lo = (rest - mid.astype(F32)).astype(BF16)
    return hi, mid, lo


def pack_kernel(place, ck, cv, sk, sv, near_out, far_out, rest_out, sem):
    core, kv = place[0], place[2]
    n = ck.shape[1]

    def copies(cache, span, out, head, first):
        return [
            pltpu.make_async_copy(cache.at[head], out.at[pl.ds(0, n)], sem.at[first]),
            pltpu.make_async_copy(span.at[head], out.at[pl.ds(n, 64)], sem.at[first + 1]),
        ]

    def move(cache, span, cache2, span2):
        mine = copies(cache, span, far_out, kv ^ 1, 0) + copies(cache, span, near_out, kv, 2)
        mine += copies(cache2, span2, rest_out, kv, 4)
        for c in mine:
            c.start()
        for c in mine:
            c.wait()

    pl.when(core == 0)(lambda: move(ck, sk, cv, sv))
    pl.when(core == 1)(lambda: move(cv, sv, ck, sk))


def pack(place, ck, cv, sk, sv):
    n = ck.shape[1] + 64
    shape = jax.ShapeDtypeStruct((n, HD), BF16)
    return pl.pallas_call(
        pack_kernel,
        out_shape=[shape] * 3,
        in_specs=[pl.BlockSpec(memory_space=pltpu.SMEM)] + [pl.BlockSpec(memory_space=pl.ANY)] * 4,
        out_specs=[pl.BlockSpec(memory_space=pltpu.VMEM)] * 3,
        scratch_shapes=[pltpu.SemaphoreType.DMA((6,))],
        compiler_params=pltpu.CompilerParams(vmem_limit_bytes=57 * MB),
        name="pack",
    )(place, ck, cv, sk, sv)


def payload_kernel(own, x, z, zx, q_ref, out_ref):
    lens = [own[0], x[0], z[0], zx[0]]
    out_ref[0:ROWS, :] = q_ref[...]
    q = q_ref[...].astype(F32)
    norm = jnp.max(jnp.sum(q * q, axis=-1, keepdims=True), axis=0, keepdims=True)
    lane = lax.broadcasted_iota(jnp.int32, (16, 128), 1)
    row = jnp.where(lane == 8, norm * 1.02, 0.0)
    for i in range(4):
        row = jnp.where(lane == 2 * i, (lens[i] // 64).astype(F32), row)
        row = jnp.where(lane == 2 * i + 1, (lens[i] % 64).astype(F32), row)
    out_ref[ROWS:ROWS + 16, :] = row.astype(BF16)


def payload(lengths, q):
    smem, vmem = pl.BlockSpec(memory_space=pltpu.SMEM), pl.BlockSpec(memory_space=pltpu.VMEM)
    return pl.pallas_call(
        payload_kernel,
        out_shape=jax.ShapeDtypeStruct((ROWS + 16, HD), BF16),
        in_specs=[smem] * 4 + [vmem],
        out_specs=vmem,
        compiler_params=pltpu.CompilerParams(vmem_limit_bytes=8 * MB),
        name="payload",
    )(*lengths, q)


def assemble_kernel(place, start, *refs):
    qs, bufs, (k_all, v_all, meta, sem) = refs[:4], refs[4:12], refs[12:]
    core, xl, z = place[0], place[1], place[3]
    sign = 1 - 2 * core
    firsts, seconds = bufs[0::2], bufs[1::2]

    def copies(keys, vals):
        pairs = [(k, k_all.at[i]) for i, k in enumerate(keys)] + [(v, v_all.at[i]) for i, v in enumerate(vals)]
        return [pltpu.make_async_copy(s, d, sem.at[i]) for i, (s, d) in enumerate(pairs)]

    def move(keys, vals):
        mine = copies(keys, vals)
        for c in mine:
            c.start()
        for c in mine:
            c.wait()

    pl.when(core == 0)(lambda: move(firsts, seconds))
    pl.when(core == 1)(lambda: move(seconds, firsts))

    lane = lax.broadcasted_iota(jnp.int32, (1, 128), 1)
    rows = [q[ROWS:ROWS + 16, :].astype(F32)[0:1, :] for q in qs]
    pick = lambda i: jnp.where(lane == 2 * i, 64.0, jnp.where(lane == 2 * i + 1, 1.0, 0.0))
    odd = lax.rem(z, 2)
    size = [jnp.sum(rows[0] * pick(i)) for i in range(4)]
    total = functools.reduce(jnp.add, rows)
    before = jnp.zeros((1, 128), F32)
    for j, row in enumerate(rows):
        at = lax.rem(z - 2 * sign * j + 2 * NZ, NZ)
        before += jnp.where(at < z, row, 0.0)
    sums = [jnp.sum(before * pick(i)) for i in range(4)]
    alls = [jnp.sum(total * pick(i)) for i in range(4)]
    low = jnp.where(xl == 0, alls[0] + alls[2], alls[1] + alls[3])
    for i in range(4):
        side, other = i % 2, i // 2
        pairs_before = sums[side] + sums[2 + side]
        own_odd = odd if other == 0 else 1 - odd
        mate = size[(2 - 2 * other) + side]
        offset = pairs_before + jnp.where(own_odd == 1, mate, 0.0)
        upper = xl if side == 0 else 1 - xl
        offset += jnp.where(upper == 1, low, 0.0)
        live = jnp.clip(start[0] - offset.astype(jnp.int32), 0, size[i].astype(jnp.int32))
        meta[i] = live
        zz = z if other == 0 else z + 1 - 2 * odd
        meta[4 + i] = (upper * NZ + zz) * 64
    meta[8] = z
    meta[9] = xl * 512
    meta[10] = sign
    q2 = jnp.sum(jnp.where(lane == 8, functools.reduce(jnp.maximum, rows), 0.0))
    ones = jnp.ones((8, HD), BF16)
    k2 = jnp.zeros((8, 1), F32)
    for i in range(4):
        k = k_all[i]
        norms = lax.dot_general(ones, k * k, (((1,), (1,)), ((), ())), preferred_element_type=F32)
        k2 = jnp.maximum(k2, jnp.max(norms, axis=-1, keepdims=True))
    meta[11] = jnp.where(q2 * jnp.max(k2) * 1.04 <= (SAFE / C2) ** 2, 1, 0).astype(jnp.int32)


def assemble(place, start, qs, bufs):
    smem, vmem = pl.BlockSpec(memory_space=pltpu.SMEM), pl.BlockSpec(memory_space=pltpu.VMEM)
    everything = jax.ShapeDtypeStruct((4,) + bufs[0].shape, BF16)
    return pl.pallas_call(
        assemble_kernel,
        out_shape=[everything, everything, jax.ShapeDtypeStruct((12,), jnp.int32)],
        in_specs=[smem, smem] + [vmem] * 4 + [pl.BlockSpec(memory_space=pl.ANY)] * 8,
        out_specs=[vmem, vmem, smem],
        scratch_shapes=[pltpu.SemaphoreType.DMA((8,))],
        compiler_params=pltpu.CompilerParams(vmem_limit_bytes=24 * MB),
        name="assemble",
    )(place, start, *qs, *bufs)


def unpack_stats(st):
    g = ROWS // 128
    return st[0:g] + st[g:2 * g] + st[2 * g:3 * g], st[3 * g:4 * g] + st[4 * g:5 * g] + st[5 * g:6 * g]


def columns(rows):
    rows = jnp.concatenate([rows, jnp.zeros((128 - rows.shape[0], 128), F32)], axis=0)
    return jnp.transpose(rows)


def attend_kernel(hop, carried, meta, *refs):
    refs = list(refs)
    take = lambda n: [refs.pop(0) for _ in range(n)]
    q_ref, k_all, v_all = take(3)
    came = take(1)[0] if carried else None
    out_ref, meta_out = take(2)
    s_ref, span_ref, m_ref, acc_ref, total_ref = refs
    for i in range(12):
        meta_out[i] = meta[i]
    z, base, sign, small = (meta[i] for i in range(8, 12))
    cache = k_all.shape[1] - 64
    ones = jnp.ones((1024, 128), BF16)
    eye = eye_mask()
    g = ROWS // 128
    token0 = base + lax.rem(z - 2 * sign * hop + 2 * NZ, NZ) * 64

    def scores_of(keys):
        return lax.dot_general(q_ref[0:ROWS, :], keys, (((1,), (1,)), ((), ())), preferred_element_type=F32)

    def span_scores():
        s = scores_of(jnp.concatenate([k_all[i, pl.ds(cache, 64), :] for i in range(4)], axis=0))
        col = lax.broadcasted_iota(jnp.int32, (1, 256), 1)
        owner = col // 64
        pos = col % 64
        for i in range(4):
            pos = jnp.where(owner == i, pos + meta[4 + i], pos)
        row = lax.broadcasted_iota(jnp.int32, s.shape, 0)
        return jnp.where(pos <= token0 + row // 8, s, NEG)

    def span_sums(p):
        values = jnp.concatenate([v_all[i, pl.ds(cache, 64), :] for i in range(4)], axis=0)
        return jnp.dot(p, jnp.concatenate([values, ones[:256]], axis=1), preferred_element_type=F32)

    @pl.when(small == 1)
    def _():
        acc_ref[...] = span_sums(jnp.exp(span_scores() * SCALE).astype(BF16))

        def shard(i, carry):
            live = meta[i]

            def piece(first, size, masked):
                def scores(j):
                    at = pl.ds(pl.multiple_of(first + j * 256, 256), 256)
                    return scores_of(k_all[i, at, :])

                total = acc_ref[...]
                ahead = scores(0)
                for j in range(size // 256):
                    s = ahead * SCALE
                    if j + 1 < size // 256:
                        ahead = scores(j + 1)
                    if masked:
                        slot = first + j * 256 + lax.broadcasted_iota(jnp.int32, (1, 256), 1)
                        s = s + jnp.where(slot < live, 0.0, NEG)
                    p = jnp.exp(s).astype(BF16)
                    at = pl.ds(pl.multiple_of(first + j * 256, 256), 256)
                    v = jnp.concatenate([v_all[i, at, :], ones[:256]], axis=1)
                    total = total + jnp.dot(p, v, preferred_element_type=F32)
                acc_ref[...] = total

            def body(t, carry):
                piece(t * 1024, 1024, False)
                return carry

            whole = live // 1024
            first = whole * 1024
            n = (live - first + 255) // 256
            lax.fori_loop(0, whole, body, 0)

            def part(t, carry):
                piece(first + t * 512, 512, True)
                return carry

            lax.fori_loop(0, n // 2, part, 0)
            pl.when(n % 2 == 1)(lambda: piece(first + (n - 1) * 256, 256, True))
            return carry

        lax.fori_loop(0, 4, shard, 0)
        m_ref[...] = jnp.where(acc_ref[:, 128:256] > 0.0, 0.0, NEG)

    @pl.when(small == 0)
    def _():
        half = lambda x: functools.reduce(jnp.maximum, [x[:, j:j + 128] for j in range(0, x.shape[1], 128)])
        s = span_scores()
        span_ref[...] = s
        m_ref[...] = half(s)

        def score_shard(i, first):
            live = meta[i]
            tiles = (live + TILE - 1) // TILE

            def score(t, carry):
                at = pl.ds(pl.multiple_of(t * TILE, TILE), TILE)
                slot = t * TILE + lax.broadcasted_iota(jnp.int32, (1, TILE), 1)
                s = scores_of(k_all[i, at, :]) + jnp.where(slot < live, 0.0, NEG)
                s_ref[first + t] = s
                m_ref[...] = jnp.maximum(m_ref[...], half(s))
                return carry

            lax.fori_loop(0, tiles, score, 0)
            return first + tiles

        lax.fori_loop(0, 4, score_shard, jnp.int32(0))
        m = jnp.broadcast_to(jnp.max(m_ref[...], axis=-1, keepdims=True), (ROWS, 128))
        m_ref[...] = m
        s = span_ref[...]
        wide = jnp.concatenate([m, m], axis=1)
        acc_ref[...] = span_sums(jnp.where(s > 0.5 * NEG, jnp.exp2((s - wide) * C2), 0.0).astype(BF16))

        def value_shard(i, first):
            tiles = (meta[i] + TILE - 1) // TILE

            def value(t, carry):
                at = pl.ds(pl.multiple_of(t * TILE, TILE), TILE)
                wide = jnp.concatenate([m_ref[...]] * (TILE // 128), axis=1)
                p = jnp.exp2((s_ref[first + t] - wide) * C2).astype(BF16)
                v = jnp.concatenate([v_all[i, at, :], ones[:TILE]], axis=1)
                acc_ref[...] += jnp.dot(p, v, preferred_element_type=F32)
                return carry

            lax.fori_loop(0, tiles, value, 0)
            return first + tiles

        lax.fori_loop(0, 4, value_shard, jnp.int32(0))

    if carried:
        ms, ls = unpack_stats(came[ROWS:ROWS + STAT, :].astype(F32))
        ft = columns(jnp.concatenate([ms, ls], axis=0))
        for r in range(g):
            at = slice(r * 128, (r + 1) * 128)
            m_in = jnp.broadcast_to(ft[:, r:r + 1], (128, 128))
            l_in = jnp.broadcast_to(ft[:, g + r:g + r + 1], (128, 128))
            m_own = m_ref[at, :]
            m = jnp.maximum(m_own, m_in)
            w_own = jnp.exp2((m_own - m) * C2)
            w_in = jnp.exp2((m_in - m) * C2) * l_in
            total = acc_ref[at, 128:256] * w_own + w_in
            mixed = acc_ref[at, 0:128] * w_own + came[at, :].astype(F32) * w_in
            out_ref[at, :] = (mixed / jnp.maximum(total, 1e-35)).astype(BF16)
            m_ref[at, :] = m
            total_ref[at, :] = total
    else:
        total = acc_ref[:, 128:256]
        out_ref[0:ROWS, :] = (acc_ref[:, 0:128] / jnp.maximum(total, 1e-35)).astype(BF16)
        total_ref[...] = total

    compact = lambda x: jnp.sum(jnp.where(eye[None], x.reshape(g, 128, 128), 0.0), axis=1)
    stats = split3(compact(m_ref[...])) + split3(compact(total_ref[...]))
    pad = jnp.zeros((STAT - 6 * g, 128), F32)
    out_ref[ROWS:ROWS + STAT, :] = jnp.concatenate([x.astype(F32) for x in stats] + [pad], axis=0).astype(BF16)


def attend(hop, meta, q, k_all, v_all, came):
    smem, vmem = pl.BlockSpec(memory_space=pltpu.SMEM), pl.BlockSpec(memory_space=pltpu.VMEM)
    tiles = 4 * (k_all.shape[1] - 64) // TILE
    came = [] if came is None else [came]
    return pl.pallas_call(
        functools.partial(attend_kernel, hop, bool(came)),
        out_shape=[jax.ShapeDtypeStruct((ROWS + STAT, 128), BF16), jax.ShapeDtypeStruct((12,), jnp.int32)],
        in_specs=[smem] + [vmem] * (3 + len(came)),
        out_specs=[vmem, smem],
        scratch_shapes=[
            pltpu.VMEM((tiles, ROWS, TILE), F32),
            pltpu.VMEM((ROWS, 256), F32),
            pltpu.VMEM((ROWS, 128), F32),
            pltpu.VMEM((ROWS, 256), F32),
            pltpu.VMEM((ROWS, 128), F32),
        ],
        compiler_params=pltpu.CompilerParams(vmem_limit_bytes=28 * MB),
        cost_estimate=pl.CostEstimate(flops=600_000_000, bytes_accessed=100_000, transcendentals=1_000),
        name="attend",
    )(meta, q, k_all, v_all, *came)


def combine_kernel(place, *refs):
    parts, (out_ref, *piece_refs, f_ref, flat_ref) = refs[:-7], refs[-7:]
    g = ROWS // 128
    ms, ls = zip(*[unpack_stats(ref[ROWS:ROWS + STAT, :].astype(F32)) for ref in parts])
    top = functools.reduce(jnp.maximum, ms)
    ws = [jnp.exp2((m - top) * C2) * l for m, l in zip(ms, ls)]
    whole = functools.reduce(jnp.add, ws)
    ft = columns(jnp.concatenate([w / whole for w in ws], axis=0))
    for r in range(g):
        total = jnp.zeros((128, 128), F32)
        for k, ref in enumerate(parts):
            total += ref[r * 128:(r + 1) * 128, :].astype(F32) * ft[:, k * g + r:k * g + r + 1]
        out_ref[r * 128:(r + 1) * 128, :] = total.astype(BF16)
        f_ref[r * 128:(r + 1) * 128, :] = total
    for h in range(8):
        flat_ref[:, h * 128:(h + 1) * 128] = f_ref[pl.ds(h, 64, stride=8), :].astype(BF16)
    core, xl = place[0], place[1]
    for i, ref in enumerate(piece_refs):
        c = core if i % 2 == 0 else 1 - core
        x = xl if i // 2 == 0 else 1 - xl
        ref[...] = flat_ref[pl.ds(pl.multiple_of(x * 32 + c * 16, 16), 16), :]


def combine(place, parts):
    vmem = pl.BlockSpec(memory_space=pltpu.VMEM)
    piece = jax.ShapeDtypeStruct((16, 1024), BF16)
    return pl.pallas_call(
        combine_kernel,
        out_shape=[jax.ShapeDtypeStruct((ROWS, 128), BF16)] + [piece] * 4,
        in_specs=[pl.BlockSpec(memory_space=pltpu.SMEM)] + [vmem] * len(parts),
        out_specs=[vmem] * 5,
        scratch_shapes=[pltpu.VMEM((ROWS, 128), F32), pltpu.VMEM((64, 1024), BF16)],
        compiler_params=pltpu.CompilerParams(vmem_limit_bytes=16 * MB),
        name="combine",
    )(place, *parts)


def local(queries, cache_keys, cache_values, span_keys, span_values, span_start, cache_lengths, out_weight):
    xl, z, y, xh, core = (lax.axis_index(a) for a in ("xl", "z", "y", "xh", "core"))
    sign = 1 - 2 * core
    kv = y * 2 + xh
    place = jnp.stack([core, xl, kv, z]).astype(jnp.int32)

    def shift(x, k):
        pairs = [(b * 2 + c, (b + k * (1 - 2 * c)) % NZ * 2 + c) for b in range(NZ) for c in range(2)]
        return lax.ppermute(x, ("z", "core"), pairs)

    swap = [(0, 1), (1, 0)]
    cross = [(i, 3 - i) for i in range(4)]
    mate = [(i, i ^ 1) for i in range(NZ)]

    both = [((a * NZ + b) * 2 + c, ((1 - a) * NZ + (b ^ 1)) * 2 + 1 - c) for a in range(2) for b in range(NZ) for c in range(2)]
    lengths = [
        cache_lengths,
        lax.ppermute(cache_lengths, ("xl", "xh"), cross),
        lax.ppermute(cache_lengths, "z", mate),
        lax.ppermute(cache_lengths, ("xl", "z", "xh"), both),
    ]

    near, far, rest = pack(place, cache_keys, cache_values, span_keys, span_values)
    near, far, lengths = lax.optimization_barrier((near, far, lengths))
    got_x = lax.ppermute(far, ("xl", "xh"), cross)
    got_z = lax.ppermute(near, "z", mate)

    q = payload(lengths, queries.reshape(ROWS, HD))
    q_blocks = [q, shift(q, 2), None, shift(q, -2)]
    got_z, q = lax.optimization_barrier((got_z, q))
    q_blocks[2] = shift(q_blocks[1], 2)
    got_zx = lax.ppermute(got_z, "xl", swap)
    got_x, got_z, got_zx, q_blocks[2], q_blocks[3], weight = lax.optimization_barrier(
        (got_x, got_z, got_zx, q_blocks[2], q_blocks[3], out_weight)
    )
    w_x1 = lax.ppermute(weight[0:768], "xl", swap)
    bufs = [near, rest]
    for got in (got_x, got_z, got_zx):
        bufs += [got, lax.ppermute(got, "core", swap)]
    k_all, v_all, meta = assemble(place, span_start, q_blocks, bufs)

    out, meta = attend(2, meta, q_blocks[2], k_all, v_all, None)
    half_way = shift(out, 2)
    out, meta = attend(1, meta, q_blocks[1], k_all, v_all, None)
    down = shift(out, -2)
    out, meta = attend(3, meta, q_blocks[3], k_all, v_all, half_way)
    up = shift(out, 2)
    own, meta = attend(0, meta, q_blocks[0], k_all, v_all, None)
    own, w_x1 = lax.optimization_barrier((own, w_x1))
    mixed, *pieces = combine(place, [own, up, down])
    attended = mixed.reshape(64, 8, HD)

    p_core = lax.ppermute(pieces[1], "core", swap)
    p_x = lax.ppermute(pieces[2], "xl", swap)
    p_both = lax.ppermute(pieces[3], ("xl", "core"), cross)
    p_core, p_x, p_both, weight = lax.optimization_barrier((p_core, p_x, p_both, weight))
    w_x2 = lax.ppermute(weight[768:1024], "xl", swap)
    w_core = lax.ppermute(weight, "core", swap)
    w_both1 = lax.ppermute(w_x1, "core", swap)
    w_both2 = lax.ppermute(w_x2, "core", swap)
    here = jnp.concatenate([pieces[0], p_core], axis=1)
    there = jnp.concatenate([p_x, p_both], axis=1)
    pair = jnp.stack([jnp.where(xl == 0, here, there), jnp.where(xl == 0, there, here)])[:, None]
    every = jnp.zeros((2, NZ, 16, 2048), BF16)
    every = lax.dynamic_update_slice(every, pair, (0, z, 0, 0))
    up = down = pair
    for k in range(1, 5):
        up = shift(up, 1)
        every = lax.dynamic_update_slice(every, up, (0, (z - sign * k + 2 * NZ) % NZ, 0, 0))
        if k < 4:
            down = shift(down, -1)
            every = lax.dynamic_update_slice(every, down, (0, (z + sign * k + 2 * NZ) % NZ, 0, 0))
    x = every.reshape(256, 2048)

    def term(*blocks):
        total, at = 0.0, 0
        for w in blocks:
            total = total + jnp.dot(x[:, at:at + w.shape[0]], w, preferred_element_type=F32)
            at += w.shape[0]
        return total.astype(BF16)

    t_own, t_peer = term(out_weight, w_core), term(w_x1, w_x2, w_both1, w_both2)
    terms = jnp.stack([jnp.where(xl == 0, t_own, t_peer), jnp.where(xl == 0, t_peer, t_own)])
    got = lax.all_to_all(terms.reshape(32, 16, 1024), ("xl", "y", "xh", "core"), 0, 0, tiled=True)
    projected = jnp.sum(got.reshape(2, 8, 2, 16, 1024).astype(F32), axis=1).astype(BF16).reshape(64, 1024)
    return attended, projected


def solution(mesh):
    fine = Mesh(mesh.devices.reshape(2, NZ, 4, 2, 2), ("xl", "z", "y", "xh", "core"))
    ctx, tp = ("xl", "z"), ("y", "xh", "core")
    return jax.shard_map(
        local,
        mesh=fine,
        in_specs=(
            P(ctx, tp, None),
            P(None, ctx, None),
            P(None, ctx, None),
            P(None, ctx, None),
            P(None, ctx, None),
            P(),
            P(ctx),
            P(tp, ctx),
        ),
        out_specs=(P(ctx, tp, None), P(tp, ctx)),
        check_vma=False,
    )
```

```python
import functools
import math

import jax
import jax.numpy as jnp
from jax import lax
from jax.experimental import pallas as pl
from jax.experimental.pallas import tpu as pltpu
from jax.sharding import Mesh, PartitionSpec as P

H = 128
KVH = 8
HD = 128
NEG = -1e30
SCALE = 1.0 / math.sqrt(HD)
C2 = math.log2(math.e) * SCALE
TILE = 256
ROWS = 512
STAT = 32
NZ = 8
SAFE = 90.0
F32 = jnp.float32
BF16 = jnp.bfloat16
MB = 1024 * 1024


def eye_mask():
    r = lax.broadcasted_iota(jnp.int32, (128, 128), 0)
    c = lax.broadcasted_iota(jnp.int32, (128, 128), 1)
    return r == c


def split3(x):
    hi = x.astype(BF16)
    rest = x - hi.astype(F32)
    mid = rest.astype(BF16)
    lo = (rest - mid.astype(F32)).astype(BF16)
    return hi, mid, lo


def pack_kernel(place, ck, cv, sk, sv, near_out, far_out, rest_out, hold, sem_in, sem_out):
    core, kv = place[0], place[2]
    n = ck.shape[1]
    step = n // 2

    def move(cache, span, cache2, span2):
        ins, outs = [], []
        for i, (src, tail, head, out) in enumerate(
            ((cache, span, kv, near_out), (cache, span, kv ^ 1, far_out), (cache2, span2, kv, rest_out))
        ):
            for j in range(3):
                at = pl.ds(j * step, step if j < 2 else 64)
                part = src.at[head, at] if j < 2 else tail.at[head]
                ins.append(pltpu.make_async_copy(part, hold.at[i, at], sem_in.at[i, j]))
                outs.append(pltpu.make_async_copy(hold.at[i, at], out.at[at], sem_out.at[i, j]))
        for c in ins:
            c.start()
        for c, d in zip(ins, outs):
            c.wait()
            d.start()
        for d in outs:
            d.wait()

    pl.when(core == 0)(lambda: move(ck, sk, cv, sv))
    pl.when(core == 1)(lambda: move(cv, sv, ck, sk))


def pack(place, ck, cv, sk, sv):
    n = ck.shape[1] + 64
    shape = jax.ShapeDtypeStruct((n, HD), BF16)
    anyspec = pl.BlockSpec(memory_space=pl.ANY)
    return pl.pallas_call(
        pack_kernel,
        out_shape=[shape] * 3,
        in_specs=[pl.BlockSpec(memory_space=pltpu.SMEM)] + [anyspec] * 4,
        out_specs=[anyspec] * 3,
        scratch_shapes=[
            pltpu.VMEM((3, n, HD), BF16),
            pltpu.SemaphoreType.DMA((3, 3)),
            pltpu.SemaphoreType.DMA((3, 3)),
        ],
        compiler_params=pltpu.CompilerParams(vmem_limit_bytes=57 * MB),
        name="pack",
    )(place, ck, cv, sk, sv)


def payload_kernel(own, x, z, zx, q_ref, out_ref):
    lens = [own[0], x[0], z[0], zx[0]]
    out_ref[0:ROWS, :] = q_ref[...]
    q = q_ref[...].astype(F32)
    norm = jnp.max(jnp.sum(q * q, axis=-1, keepdims=True), axis=0, keepdims=True)
    lane = lax.broadcasted_iota(jnp.int32, (16, 128), 1)
    row = jnp.where(lane == 8, norm * 1.02, 0.0)
    for i in range(4):
        row = jnp.where(lane == 2 * i, (lens[i] // 64).astype(F32), row)
        row = jnp.where(lane == 2 * i + 1, (lens[i] % 64).astype(F32), row)
    out_ref[ROWS:ROWS + 16, :] = row.astype(BF16)


def payload(lengths, q):
    smem, vmem = pl.BlockSpec(memory_space=pltpu.SMEM), pl.BlockSpec(memory_space=pltpu.VMEM)
    return pl.pallas_call(
        payload_kernel,
        out_shape=jax.ShapeDtypeStruct((ROWS + 16, HD), BF16),
        in_specs=[smem] * 4 + [vmem],
        out_specs=vmem,
        compiler_params=pltpu.CompilerParams(vmem_limit_bytes=8 * MB),
        name="payload",
    )(*lengths, q)


def assemble_kernel(place, start, *refs):
    qs, bufs, (kt_all, k_span, v_all, meta, k_all, sem) = refs[:4], refs[4:12], refs[12:]
    core, xl, z = place[0], place[1], place[3]
    sign = 1 - 2 * core
    firsts, seconds = bufs[0::2], bufs[1::2]

    def copies(keys, vals):
        pairs = [(k, k_all.at[i]) for i, k in enumerate(keys)] + [(v, v_all.at[i]) for i, v in enumerate(vals)]
        return [pltpu.make_async_copy(s, d, sem.at[i]) for i, (s, d) in enumerate(pairs)]

    def move(keys, vals):
        mine = copies(keys, vals)
        for c in mine:
            c.start()
        for c in mine:
            c.wait()

    pl.when(core == 0)(lambda: move(firsts, seconds))
    pl.when(core == 1)(lambda: move(seconds, firsts))

    lane = lax.broadcasted_iota(jnp.int32, (1, 128), 1)
    rows = [q[ROWS:ROWS + 16, :].astype(F32)[0:1, :] for q in qs]
    pick = lambda i: jnp.where(lane == 2 * i, 64.0, jnp.where(lane == 2 * i + 1, 1.0, 0.0))
    odd = lax.rem(z, 2)
    size = [jnp.sum(rows[0] * pick(i)) for i in range(4)]
    total = functools.reduce(jnp.add, rows)
    before = jnp.zeros((1, 128), F32)
    for j, row in enumerate(rows):
        at = lax.rem(z - 2 * sign * j + 2 * NZ, NZ)
        before += jnp.where(at < z, row, 0.0)
    sums = [jnp.sum(before * pick(i)) for i in range(4)]
    alls = [jnp.sum(total * pick(i)) for i in range(4)]
    low = jnp.where(xl == 0, alls[0] + alls[2], alls[1] + alls[3])
    for i in range(4):
        side, other = i % 2, i // 2
        pairs_before = sums[side] + sums[2 + side]
        own_odd = odd if other == 0 else 1 - odd
        mate = size[(2 - 2 * other) + side]
        offset = pairs_before + jnp.where(own_odd == 1, mate, 0.0)
        upper = xl if side == 0 else 1 - xl
        offset += jnp.where(upper == 1, low, 0.0)
        live = jnp.clip(start[0] - offset.astype(jnp.int32), 0, size[i].astype(jnp.int32))
        meta[i] = live
        zz = z if other == 0 else z + 1 - 2 * odd
        meta[4 + i] = (upper * NZ + zz) * 64
    meta[8] = z
    meta[9] = xl * 512
    meta[10] = sign
    q2 = jnp.sum(jnp.where(lane == 8, functools.reduce(jnp.maximum, rows), 0.0))
    n = kt_all.shape[2]
    k2 = jnp.zeros((1, n), F32)
    for i in range(4):
        kt = jnp.transpose(k_all[i, 0:n, :])
        kt_all[i] = kt
        kf = kt.astype(F32)
        k2 = jnp.maximum(k2, jnp.sum(kf * kf, axis=0, keepdims=True))
        tail = k_all[i, pl.ds(n, 64), :]
        k_span[i * 64:(i + 1) * 64, :] = tail
    tails = k_span[...].astype(F32)
    k2 = jnp.maximum(jnp.max(k2), jnp.max(jnp.sum(tails * tails, axis=-1, keepdims=True)))
    meta[11] = jnp.where(q2 * k2 * 1.04 <= (SAFE / C2) ** 2, 1, 0).astype(jnp.int32)


def assemble(place, start, qs, bufs):
    smem, vmem = pl.BlockSpec(memory_space=pltpu.SMEM), pl.BlockSpec(memory_space=pltpu.VMEM)
    n = bufs[0].shape[0]
    everything = jax.ShapeDtypeStruct((4, n, HD), BF16)
    turned = jax.ShapeDtypeStruct((4, HD, n - 64), BF16)
    tails = jax.ShapeDtypeStruct((256, HD), BF16)
    return pl.pallas_call(
        assemble_kernel,
        out_shape=[turned, tails, everything, jax.ShapeDtypeStruct((12,), jnp.int32)],
        in_specs=[smem, smem] + [vmem] * 4 + [pl.BlockSpec(memory_space=pl.ANY)] * 8,
        out_specs=[vmem, vmem, vmem, smem],
        scratch_shapes=[pltpu.VMEM((4, n, HD), BF16), pltpu.SemaphoreType.DMA((8,))],
        compiler_params=pltpu.CompilerParams(vmem_limit_bytes=24 * MB),
        name="assemble",
    )(place, start, *qs, *bufs)


def unpack_stats(st):
    g = ROWS // 128
    return st[0:g] + st[g:2 * g] + st[2 * g:3 * g], st[3 * g:4 * g] + st[4 * g:5 * g] + st[5 * g:6 * g]


def columns(rows):
    rows = jnp.concatenate([rows, jnp.zeros((128 - rows.shape[0], 128), F32)], axis=0)
    return jnp.transpose(rows)


def attend_kernel(hop, carried, meta, *refs):
    refs = list(refs)
    take = lambda n: [refs.pop(0) for _ in range(n)]
    q_ref, kt_all, k_span, v_all = take(4)
    came = take(1)[0] if carried else None
    out_ref, meta_out = take(2)
    s_ref, span_ref, m_ref, acc_ref, total_ref = refs
    for i in range(12):
        meta_out[i] = meta[i]
    z, base, sign, small = (meta[i] for i in range(8, 12))
    cache = kt_all.shape[2]
    ones = jnp.ones((256, 128), BF16)
    eye = eye_mask()
    g = ROWS // 128
    token0 = base + lax.rem(z - 2 * sign * hop + 2 * NZ, NZ) * 64

    def scores_of(turned):
        return jnp.dot(q_ref[0:ROWS, :], turned, preferred_element_type=F32)

    def span_scores():
        s = lax.dot_general(q_ref[0:ROWS, :], k_span[...], (((1,), (1,)), ((), ())), preferred_element_type=F32)
        col = lax.broadcasted_iota(jnp.int32, (1, 256), 1)
        owner = col // 64
        pos = col % 64
        for i in range(4):
            pos = jnp.where(owner == i, pos + meta[4 + i], pos)
        row = lax.broadcasted_iota(jnp.int32, s.shape, 0)
        return jnp.where(pos <= token0 + row // 8, s, NEG)

    def span_sums(p):
        values = jnp.concatenate([v_all[i, pl.ds(cache, 64), :] for i in range(4)], axis=0)
        return jnp.dot(p, jnp.concatenate([values, ones], axis=1), preferred_element_type=F32)

    @pl.when(small == 1)
    def _():
        acc_ref[...] = span_sums(jnp.exp(span_scores() * SCALE).astype(BF16))

        def shard(i, carry):
            live = meta[i]

            def piece(first, size, masked):
                def scores(j):
                    at = pl.ds(pl.multiple_of(first + j * 256, 256), 256)
                    return scores_of(kt_all[i, :, at])

                total = acc_ref[...]
                ahead = scores(0)
                for j in range(size // 256):
                    s = ahead * SCALE
                    if j + 1 < size // 256:
                        ahead = scores(j + 1)
                    if masked:
                        slot = first + j * 256 + lax.broadcasted_iota(jnp.int32, (1, 256), 1)
                        s = s + jnp.where(slot < live, 0.0, NEG)
                    p = jnp.exp(s).astype(BF16)
                    at = pl.ds(pl.multiple_of(first + j * 256, 256), 256)
                    v = jnp.concatenate([v_all[i, at, :], ones], axis=1)
                    total = total + jnp.dot(p, v, preferred_element_type=F32)
                acc_ref[...] = total

            def body(t, carry):
                piece(t * 1024, 1024, False)
                return carry

            whole = live // 1024
            first = whole * 1024
            n = (live - first + 255) // 256
            lax.fori_loop(0, whole, body, 0)

            def part(t, carry):
                piece(first + t * 512, 512, True)
                return carry

            lax.fori_loop(0, n // 2, part, 0)
            pl.when(n % 2 == 1)(lambda: piece(first + (n - 1) * 256, 256, True))
            return carry

        lax.fori_loop(0, 4, shard, 0)
        m_ref[...] = jnp.where(acc_ref[:, 128:256] > 0.0, 0.0, NEG)

    @pl.when(small == 0)
    def _():
        half = lambda x: functools.reduce(jnp.maximum, [x[:, j:j + 128] for j in range(0, x.shape[1], 128)])
        s = span_scores()
        span_ref[...] = s
        m_ref[...] = half(s)

        def score_shard(i, first):
            live = meta[i]
            tiles = (live + TILE - 1) // TILE

            def score(t, carry):
                at = pl.ds(pl.multiple_of(t * TILE, TILE), TILE)
                slot = t * TILE + lax.broadcasted_iota(jnp.int32, (1, TILE), 1)
                s = scores_of(kt_all[i, :, at]) + jnp.where(slot < live, 0.0, NEG)
                s_ref[first + t] = s
                m_ref[...] = jnp.maximum(m_ref[...], half(s))
                return carry

            lax.fori_loop(0, tiles, score, 0)
            return first + tiles

        lax.fori_loop(0, 4, score_shard, jnp.int32(0))
        m = jnp.broadcast_to(jnp.max(m_ref[...], axis=-1, keepdims=True), (ROWS, 128))
        m_ref[...] = m
        s = span_ref[...]
        wide = jnp.concatenate([m, m], axis=1)
        acc_ref[...] = span_sums(jnp.where(s > 0.5 * NEG, jnp.exp2((s - wide) * C2), 0.0).astype(BF16))

        def value_shard(i, first):
            tiles = (meta[i] + TILE - 1) // TILE

            def value(t, carry):
                at = pl.ds(pl.multiple_of(t * TILE, TILE), TILE)
                wide = jnp.concatenate([m_ref[...]] * (TILE // 128), axis=1)
                p = jnp.exp2((s_ref[first + t] - wide) * C2).astype(BF16)
                v = jnp.concatenate([v_all[i, at, :], ones], axis=1)
                acc_ref[...] += jnp.dot(p, v, preferred_element_type=F32)
                return carry

            lax.fori_loop(0, tiles, value, 0)
            return first + tiles

        lax.fori_loop(0, 4, value_shard, jnp.int32(0))

    if carried:
        ms, ls = unpack_stats(came[ROWS:ROWS + STAT, :].astype(F32))
        ft = columns(jnp.concatenate([ms, ls], axis=0))
        for r in range(g):
            at = slice(r * 128, (r + 1) * 128)
            m_in = jnp.broadcast_to(ft[:, r:r + 1], (128, 128))
            l_in = jnp.broadcast_to(ft[:, g + r:g + r + 1], (128, 128))
            m_own = m_ref[at, :]
            m = jnp.maximum(m_own, m_in)
            w_own = jnp.exp2((m_own - m) * C2)
            w_in = jnp.exp2((m_in - m) * C2) * l_in
            total = acc_ref[at, 128:256] * w_own + w_in
            mixed = acc_ref[at, 0:128] * w_own + came[at, :].astype(F32) * w_in
            out_ref[at, :] = (mixed / jnp.maximum(total, 1e-35)).astype(BF16)
            m_ref[at, :] = m
            total_ref[at, :] = total
    else:
        total = acc_ref[:, 128:256]
        out_ref[0:ROWS, :] = (acc_ref[:, 0:128] / jnp.maximum(total, 1e-35)).astype(BF16)
        total_ref[...] = total

    compact = lambda x: jnp.sum(jnp.where(eye[None], x.reshape(g, 128, 128), 0.0), axis=1)
    stats = split3(compact(m_ref[...])) + split3(compact(total_ref[...]))
    pad = jnp.zeros((STAT - 6 * g, 128), F32)
    out_ref[ROWS:ROWS + STAT, :] = jnp.concatenate([x.astype(F32) for x in stats] + [pad], axis=0).astype(BF16)


def attend(hop, meta, q, kv_all, came):
    smem, vmem = pl.BlockSpec(memory_space=pltpu.SMEM), pl.BlockSpec(memory_space=pltpu.VMEM)
    tiles = 4 * kv_all[0].shape[2] // TILE
    came = [] if came is None else [came]
    return pl.pallas_call(
        functools.partial(attend_kernel, hop, bool(came)),
        out_shape=[jax.ShapeDtypeStruct((ROWS + STAT, 128), BF16), jax.ShapeDtypeStruct((12,), jnp.int32)],
        in_specs=[smem] + [vmem] * (4 + len(came)),
        out_specs=[vmem, smem],
        scratch_shapes=[
            pltpu.VMEM((tiles, ROWS, TILE), F32),
            pltpu.VMEM((ROWS, 256), F32),
            pltpu.VMEM((ROWS, 128), F32),
            pltpu.VMEM((ROWS, 256), F32),
            pltpu.VMEM((ROWS, 128), F32),
        ],
        compiler_params=pltpu.CompilerParams(vmem_limit_bytes=28 * MB),
        cost_estimate=pl.CostEstimate(flops=600_000_000, bytes_accessed=100_000, transcendentals=1_000),
        name="attend",
    )(meta, q, *kv_all, *came)


def combine_kernel(place, *refs):
    parts, (out_ref, *piece_refs, f_ref, flat_ref) = refs[:-7], refs[-7:]
    g = ROWS // 128
    ms, ls = zip(*[unpack_stats(ref[ROWS:ROWS + STAT, :].astype(F32)) for ref in parts])
    top = functools.reduce(jnp.maximum, ms)
    ws = [jnp.exp2((m - top) * C2) * l for m, l in zip(ms, ls)]
    whole = functools.reduce(jnp.add, ws)
    ft = columns(jnp.concatenate([w / whole for w in ws], axis=0))
    for r in range(g):
        total = jnp.zeros((128, 128), F32)
        for k, ref in enumerate(parts):
            total += ref[r * 128:(r + 1) * 128, :].astype(F32) * ft[:, k * g + r:k * g + r + 1]
        out_ref[r * 128:(r + 1) * 128, :] = total.astype(BF16)
        f_ref[r * 128:(r + 1) * 128, :] = total
    for h in range(8):
        flat_ref[:, h * 128:(h + 1) * 128] = f_ref[pl.ds(h, 64, stride=8), :].astype(BF16)
    core, xl = place[0], place[1]
    for i, ref in enumerate(piece_refs):
        c = core if i % 2 == 0 else 1 - core
        x = xl if i // 2 == 0 else 1 - xl
        ref[...] = flat_ref[pl.ds(pl.multiple_of(x * 32 + c * 16, 16), 16), :]


def combine(place, parts):
    vmem = pl.BlockSpec(memory_space=pltpu.VMEM)
    piece = jax.ShapeDtypeStruct((16, 1024), BF16)
    return pl.pallas_call(
        combine_kernel,
        out_shape=[jax.ShapeDtypeStruct((ROWS, 128), BF16)] + [piece] * 4,
        in_specs=[pl.BlockSpec(memory_space=pltpu.SMEM)] + [vmem] * len(parts),
        out_specs=[vmem] * 5,
        scratch_shapes=[pltpu.VMEM((ROWS, 128), F32), pltpu.VMEM((64, 1024), BF16)],
        compiler_params=pltpu.CompilerParams(vmem_limit_bytes=16 * MB),
        name="combine",
    )(place, *parts)


def local(queries, cache_keys, cache_values, span_keys, span_values, span_start, cache_lengths, out_weight):
    xl, z, y, xh, core = (lax.axis_index(a) for a in ("xl", "z", "y", "xh", "core"))
    sign = 1 - 2 * core
    kv = y * 2 + xh
    place = jnp.stack([core, xl, kv, z]).astype(jnp.int32)

    def shift(x, k):
        pairs = [(b * 2 + c, (b + k * (1 - 2 * c)) % NZ * 2 + c) for b in range(NZ) for c in range(2)]
        return lax.ppermute(x, ("z", "core"), pairs)

    swap = [(0, 1), (1, 0)]
    cross = [(i, 3 - i) for i in range(4)]
    mate = [(i, i ^ 1) for i in range(NZ)]

    both = [((a * NZ + b) * 2 + c, ((1 - a) * NZ + (b ^ 1)) * 2 + 1 - c) for a in range(2) for b in range(NZ) for c in range(2)]
    lengths = [
        cache_lengths,
        lax.ppermute(cache_lengths, ("xl", "xh"), cross),
        lax.ppermute(cache_lengths, "z", mate),
        lax.ppermute(cache_lengths, ("xl", "z", "xh"), both),
    ]

    near, far, rest = pack(place, cache_keys, cache_values, span_keys, span_values)
    near, far, lengths = lax.optimization_barrier((near, far, lengths))
    got_x = lax.ppermute(far, ("xl", "xh"), cross)
    got_z = lax.ppermute(near, "z", mate)

    q = payload(lengths, queries.reshape(ROWS, HD))
    q_blocks = [q, shift(q, 2), None, shift(q, -2)]
    q_blocks[2] = shift(q_blocks[1], 2)
    got_zx = lax.ppermute(got_z, "xl", swap)
    bufs = [near, rest]
    for got in (got_x, got_z):
        bufs += [got, lax.ppermute(got, "core", swap)]
    got_zx, q_blocks[2], q_blocks[3], bufs, weight = lax.optimization_barrier(
        (got_zx, q_blocks[2], q_blocks[3], bufs, out_weight)
    )
    bufs += [got_zx, lax.ppermute(got_zx, "core", swap)]
    w_x1 = lax.ppermute(weight[0:768], "xl", swap)
    *kv_all, meta = assemble(place, span_start, q_blocks, bufs)

    out, meta = attend(2, meta, q_blocks[2], kv_all, None)
    half_way = shift(out, 2)
    out, meta = attend(1, meta, q_blocks[1], kv_all, None)
    down = shift(out, -2)
    out, meta = attend(3, meta, q_blocks[3], kv_all, half_way)
    up = shift(out, 2)
    own, meta = attend(0, meta, q_blocks[0], kv_all, None)
    own, w_x1 = lax.optimization_barrier((own, w_x1))
    mixed, *pieces = combine(place, [own, up, down])
    attended = mixed.reshape(64, 8, HD)

    p_core = lax.ppermute(pieces[1], "core", swap)
    p_x = lax.ppermute(pieces[2], "xl", swap)
    p_both = lax.ppermute(pieces[3], ("xl", "core"), cross)
    p_core, p_x, p_both, weight = lax.optimization_barrier((p_core, p_x, p_both, weight))
    w_x2 = lax.ppermute(weight[768:1024], "xl", swap)
    w_core = lax.ppermute(weight, "core", swap)
    w_both1 = lax.ppermute(w_x1, "core", swap)
    w_both2 = lax.ppermute(w_x2, "core", swap)
    here = jnp.concatenate([pieces[0], p_core], axis=1)
    there = jnp.concatenate([p_x, p_both], axis=1)
    pair = jnp.stack([jnp.where(xl == 0, here, there), jnp.where(xl == 0, there, here)])[:, None]
    every = jnp.zeros((2, NZ, 16, 2048), BF16)
    every = lax.dynamic_update_slice(every, pair, (0, z, 0, 0))
    up = down = pair
    for k in range(1, 5):
        up = shift(up, 1)
        every = lax.dynamic_update_slice(every, up, (0, (z - sign * k + 2 * NZ) % NZ, 0, 0))
        if k < 4:
            down = shift(down, -1)
            every = lax.dynamic_update_slice(every, down, (0, (z + sign * k + 2 * NZ) % NZ, 0, 0))
    x = every.reshape(256, 2048)

    def term(*blocks):
        total, at = 0.0, 0
        for w in blocks:
            total = total + jnp.dot(x[:, at:at + w.shape[0]], w, preferred_element_type=F32)
            at += w.shape[0]
        return total.astype(BF16)

    t_own, t_peer = term(out_weight, w_core), term(w_x1, w_x2, w_both1, w_both2)
    terms = jnp.stack([jnp.where(xl == 0, t_own, t_peer), jnp.where(xl == 0, t_peer, t_own)])
    got = lax.all_to_all(terms.reshape(32, 16, 1024), ("xl", "y", "xh", "core"), 0, 0, tiled=True)
    projected = jnp.sum(got.reshape(2, 8, 2, 16, 1024).astype(F32), axis=1).astype(BF16).reshape(64, 1024)
    return attended, projected


def solution(mesh):
    fine = Mesh(mesh.devices.reshape(2, NZ, 4, 2, 2), ("xl", "z", "y", "xh", "core"))
    ctx, tp = ("xl", "z"), ("y", "xh", "core")
    return jax.shard_map(
        local,
        mesh=fine,
        in_specs=(
            P(ctx, tp, None),
            P(None, ctx, None),
            P(None, ctx, None),
            P(None, ctx, None),
            P(None, ctx, None),
            P(),
            P(ctx),
            P(tp, ctx),
        ),
        out_specs=(P(ctx, tp, None), P(tp, ctx)),
        check_vma=False,
    )
```

```python
import functools
import math

import jax
import jax.numpy as jnp
from jax import lax
from jax.experimental import pallas as pl
from jax.experimental.pallas import tpu as pltpu
from jax.sharding import Mesh, PartitionSpec as P

H = 128
KVH = 8
HD = 128
NEG = -1e30
SCALE = 1.0 / math.sqrt(HD)
C2 = math.log2(math.e) * SCALE
TILE = 256
ROWS = 512
STAT = 32
NZ = 8
SAFE = 90.0
F32 = jnp.float32
BF16 = jnp.bfloat16
MB = 1024 * 1024


def eye_mask():
    r = lax.broadcasted_iota(jnp.int32, (128, 128), 0)
    c = lax.broadcasted_iota(jnp.int32, (128, 128), 1)
    return r == c


def split3(x):
    hi = x.astype(BF16)
    rest = x - hi.astype(F32)
    mid = rest.astype(BF16)
    lo = (rest - mid.astype(F32)).astype(BF16)
    return hi, mid, lo


def pack_kernel(place, ck, cv, sk, sv, near_out, far_out, rest_out, hold, sem_in, sem_out):
    core, kv = place[0], place[2]
    n = ck.shape[1]
    step = n // 2

    def move(cache, span, cache2, span2):
        ins, outs = [], []
        for i, (src, tail, head, out) in enumerate(
            ((cache, span, kv, near_out), (cache, span, kv ^ 1, far_out), (cache2, span2, kv, rest_out))
        ):
            for j in range(3):
                at = pl.ds(j * step, step if j < 2 else 64)
                part = src.at[head, at] if j < 2 else tail.at[head]
                ins.append(pltpu.make_async_copy(part, hold.at[i, at], sem_in.at[i, j]))
                outs.append(pltpu.make_async_copy(hold.at[i, at], out.at[at], sem_out.at[i, j]))
        for c in ins:
            c.start()
        for c, d in zip(ins, outs):
            c.wait()
            d.start()
        for d in outs:
            d.wait()

    pl.when(core == 0)(lambda: move(ck, sk, cv, sv))
    pl.when(core == 1)(lambda: move(cv, sv, ck, sk))


def pack(place, ck, cv, sk, sv):
    n = ck.shape[1] + 64
    shape = jax.ShapeDtypeStruct((n, HD), BF16)
    anyspec = pl.BlockSpec(memory_space=pl.ANY)
    return pl.pallas_call(
        pack_kernel,
        out_shape=[shape] * 3,
        in_specs=[pl.BlockSpec(memory_space=pltpu.SMEM)] + [anyspec] * 4,
        out_specs=[anyspec] * 3,
        scratch_shapes=[
            pltpu.VMEM((3, n, HD), BF16),
            pltpu.SemaphoreType.DMA((3, 3)),
            pltpu.SemaphoreType.DMA((3, 3)),
        ],
        compiler_params=pltpu.CompilerParams(vmem_limit_bytes=57 * MB),
        name="pack",
    )(place, ck, cv, sk, sv)


def payload_kernel(own, x, z, zx, q_ref, out_ref):
    lens = [own[0], x[0], z[0], zx[0]]
    out_ref[0:ROWS, :] = q_ref[...]
    q = q_ref[...].astype(F32)
    norm = jnp.max(jnp.sum(q * q, axis=-1, keepdims=True), axis=0, keepdims=True)
    lane = lax.broadcasted_iota(jnp.int32, (16, 128), 1)
    row = jnp.where(lane == 8, norm * 1.02, 0.0)
    for i in range(4):
        row = jnp.where(lane == 2 * i, (lens[i] // 64).astype(F32), row)
        row = jnp.where(lane == 2 * i + 1, (lens[i] % 64).astype(F32), row)
    out_ref[ROWS:ROWS + 16, :] = row.astype(BF16)


def payload(lengths, q):
    smem, vmem = pl.BlockSpec(memory_space=pltpu.SMEM), pl.BlockSpec(memory_space=pltpu.VMEM)
    return pl.pallas_call(
        payload_kernel,
        out_shape=jax.ShapeDtypeStruct((ROWS + 16, HD), BF16),
        in_specs=[smem] * 4 + [vmem],
        out_specs=vmem,
        compiler_params=pltpu.CompilerParams(vmem_limit_bytes=8 * MB),
        name="payload",
    )(*lengths, q)


def assemble_kernel(place, start, *refs):
    qs, bufs, (kt_all, k_span, v_all, meta, k_all, sem) = refs[:4], refs[4:12], refs[12:]
    core, xl, z = place[0], place[1], place[3]
    sign = 1 - 2 * core
    firsts, seconds = bufs[0::2], bufs[1::2]

    def copies(keys, vals):
        pairs = [(k, k_all.at[i]) for i, k in enumerate(keys)] + [(v, v_all.at[i]) for i, v in enumerate(vals)]
        return [pltpu.make_async_copy(s, d, sem.at[i]) for i, (s, d) in enumerate(pairs)]

    def move(keys, vals):
        mine = copies(keys, vals)
        for c in mine:
            c.start()
        for c in mine:
            c.wait()

    pl.when(core == 0)(lambda: move(firsts, seconds))
    pl.when(core == 1)(lambda: move(seconds, firsts))

    lane = lax.broadcasted_iota(jnp.int32, (1, 128), 1)
    rows = [q[ROWS:ROWS + 16, :].astype(F32)[0:1, :] for q in qs]
    pick = lambda i: jnp.where(lane == 2 * i, 64.0, jnp.where(lane == 2 * i + 1, 1.0, 0.0))
    odd = lax.rem(z, 2)
    size = [jnp.sum(rows[0] * pick(i)) for i in range(4)]
    total = functools.reduce(jnp.add, rows)
    before = jnp.zeros((1, 128), F32)
    for j, row in enumerate(rows):
        at = lax.rem(z - 2 * sign * j + 2 * NZ, NZ)
        before += jnp.where(at < z, row, 0.0)
    sums = [jnp.sum(before * pick(i)) for i in range(4)]
    alls = [jnp.sum(total * pick(i)) for i in range(4)]
    low = jnp.where(xl == 0, alls[0] + alls[2], alls[1] + alls[3])
    for i in range(4):
        side, other = i % 2, i // 2
        pairs_before = sums[side] + sums[2 + side]
        own_odd = odd if other == 0 else 1 - odd
        mate = size[(2 - 2 * other) + side]
        offset = pairs_before + jnp.where(own_odd == 1, mate, 0.0)
        upper = xl if side == 0 else 1 - xl
        offset += jnp.where(upper == 1, low, 0.0)
        live = jnp.clip(start[0] - offset.astype(jnp.int32), 0, size[i].astype(jnp.int32))
        meta[i] = live
        zz = z if other == 0 else z + 1 - 2 * odd
        meta[4 + i] = (upper * NZ + zz) * 64
    meta[8] = z
    meta[9] = xl * 512
    meta[10] = sign
    q2 = jnp.sum(jnp.where(lane == 8, functools.reduce(jnp.maximum, rows), 0.0))
    n = kt_all.shape[2]
    k2 = jnp.zeros((1, n), F32)
    for i in range(4):
        kt = jnp.transpose(k_all[i, 0:n, :])
        kt_all[i] = kt
        kf = kt.astype(F32)
        k2 = jnp.maximum(k2, jnp.sum(kf * kf, axis=0, keepdims=True))
        tail = k_all[i, pl.ds(n, 64), :]
        k_span[i * 64:(i + 1) * 64, :] = tail
    tails = k_span[...].astype(F32)
    k2 = jnp.maximum(jnp.max(k2), jnp.max(jnp.sum(tails * tails, axis=-1, keepdims=True)))
    meta[11] = jnp.where(q2 * k2 * 1.04 <= (SAFE / C2) ** 2, 1, 0).astype(jnp.int32)


def assemble(place, start, qs, bufs):
    smem, vmem = pl.BlockSpec(memory_space=pltpu.SMEM), pl.BlockSpec(memory_space=pltpu.VMEM)
    n = bufs[0].shape[0]
    everything = jax.ShapeDtypeStruct((4, n, HD), BF16)
    turned = jax.ShapeDtypeStruct((4, HD, n - 64), BF16)
    tails = jax.ShapeDtypeStruct((256, HD), BF16)
    return pl.pallas_call(
        assemble_kernel,
        out_shape=[turned, tails, everything, jax.ShapeDtypeStruct((12,), jnp.int32)],
        in_specs=[smem, smem] + [vmem] * 4 + [pl.BlockSpec(memory_space=pl.ANY)] * 8,
        out_specs=[vmem, vmem, vmem, smem],
        scratch_shapes=[pltpu.VMEM((4, n, HD), BF16), pltpu.SemaphoreType.DMA((8,))],
        compiler_params=pltpu.CompilerParams(vmem_limit_bytes=24 * MB),
        name="assemble",
    )(place, start, *qs, *bufs)


def unpack_stats(st):
    g = ROWS // 128
    return st[0:g] + st[g:2 * g] + st[2 * g:3 * g], st[3 * g:4 * g] + st[4 * g:5 * g] + st[5 * g:6 * g]


def columns(rows):
    rows = jnp.concatenate([rows, jnp.zeros((128 - rows.shape[0], 128), F32)], axis=0)
    return jnp.transpose(rows)


def attend_kernel(hop, carried, meta, *refs):
    refs = list(refs)
    take = lambda n: [refs.pop(0) for _ in range(n)]
    q_ref, kt_all, k_span, v_all = take(4)
    came = take(1)[0] if carried else None
    out_ref, meta_out = take(2)
    s_ref, span_ref, m_ref, acc_ref, total_ref = refs
    for i in range(12):
        meta_out[i] = meta[i]
    z, base, sign, small = (meta[i] for i in range(8, 12))
    cache = kt_all.shape[2]
    ones = jnp.ones((256, 128), BF16)
    eye = eye_mask()
    g = ROWS // 128
    token0 = base + lax.rem(z - 2 * sign * hop + 2 * NZ, NZ) * 64

    def scores_of(turned):
        return jnp.dot(q_ref[0:ROWS, :], turned, preferred_element_type=F32)

    def span_scores():
        s = lax.dot_general(q_ref[0:ROWS, :], k_span[...], (((1,), (1,)), ((), ())), preferred_element_type=F32)
        col = lax.broadcasted_iota(jnp.int32, (1, 256), 1)
        owner = col // 64
        pos = col % 64
        for i in range(4):
            pos = jnp.where(owner == i, pos + meta[4 + i], pos)
        row = lax.broadcasted_iota(jnp.int32, s.shape, 0)
        return jnp.where(pos <= token0 + row // 8, s, NEG)

    def span_sums(p):
        values = jnp.concatenate([v_all[i, pl.ds(cache, 64), :] for i in range(4)], axis=0)
        return jnp.dot(p, jnp.concatenate([values, ones], axis=1), preferred_element_type=F32)

    @pl.when(small == 1)
    def _():
        acc_ref[...] = span_sums(jnp.exp(span_scores() * SCALE).astype(BF16))

        def shard(i, carry):
            live = meta[i]

            def piece(first, size, masked):
                def scores(j):
                    at = pl.ds(pl.multiple_of(first + j * 256, 256), 256)
                    return scores_of(kt_all[i, :, at])

                total = acc_ref[...]
                ahead = scores(0)
                for j in range(size // 256):
                    s = ahead * SCALE
                    if j + 1 < size // 256:
                        ahead = scores(j + 1)
                    if masked:
                        slot = first + j * 256 + lax.broadcasted_iota(jnp.int32, (1, 256), 1)
                        s = s + jnp.where(slot < live, 0.0, NEG)
                    p = jnp.exp(s).astype(BF16)
                    at = pl.ds(pl.multiple_of(first + j * 256, 256), 256)
                    v = jnp.concatenate([v_all[i, at, :], ones], axis=1)
                    total = total + jnp.dot(p, v, preferred_element_type=F32)
                acc_ref[...] = total

            def body(t, carry):
                piece(t * 1024, 1024, False)
                return carry

            whole = live // 1024
            first = whole * 1024
            n = (live - first + 255) // 256
            lax.fori_loop(0, whole, body, 0)

            def part(t, carry):
                piece(first + t * 512, 512, True)
                return carry

            lax.fori_loop(0, n // 2, part, 0)
            pl.when(n % 2 == 1)(lambda: piece(first + (n - 1) * 256, 256, True))
            return carry

        lax.fori_loop(0, 4, shard, 0)
        m_ref[...] = jnp.where(acc_ref[:, 128:256] > 0.0, 0.0, NEG)

    @pl.when(small == 0)
    def _():
        half = lambda x: functools.reduce(jnp.maximum, [x[:, j:j + 128] for j in range(0, x.shape[1], 128)])
        s = span_scores()
        span_ref[...] = s
        m_ref[...] = half(s)

        def score_shard(i, first):
            live = meta[i]
            tiles = (live + TILE - 1) // TILE

            def score(t, carry):
                at = pl.ds(pl.multiple_of(t * TILE, TILE), TILE)
                slot = t * TILE + lax.broadcasted_iota(jnp.int32, (1, TILE), 1)
                s = scores_of(kt_all[i, :, at]) + jnp.where(slot < live, 0.0, NEG)
                s_ref[first + t] = s
                m_ref[...] = jnp.maximum(m_ref[...], half(s))
                return carry

            lax.fori_loop(0, tiles, score, 0)
            return first + tiles

        lax.fori_loop(0, 4, score_shard, jnp.int32(0))
        m = jnp.broadcast_to(jnp.max(m_ref[...], axis=-1, keepdims=True), (ROWS, 128))
        m_ref[...] = m
        s = span_ref[...]
        wide = jnp.concatenate([m, m], axis=1)
        acc_ref[...] = span_sums(jnp.where(s > 0.5 * NEG, jnp.exp2((s - wide) * C2), 0.0).astype(BF16))

        def value_shard(i, first):
            tiles = (meta[i] + TILE - 1) // TILE

            def value(t, carry):
                at = pl.ds(pl.multiple_of(t * TILE, TILE), TILE)
                wide = jnp.concatenate([m_ref[...]] * (TILE // 128), axis=1)
                p = jnp.exp2((s_ref[first + t] - wide) * C2).astype(BF16)
                v = jnp.concatenate([v_all[i, at, :], ones], axis=1)
                acc_ref[...] += jnp.dot(p, v, preferred_element_type=F32)
                return carry

            lax.fori_loop(0, tiles, value, 0)
            return first + tiles

        lax.fori_loop(0, 4, value_shard, jnp.int32(0))

    if carried:
        ms, ls = unpack_stats(came[ROWS:ROWS + STAT, :].astype(F32))
        ft = columns(jnp.concatenate([ms, ls], axis=0))
        for r in range(g):
            at = slice(r * 128, (r + 1) * 128)
            m_in = jnp.broadcast_to(ft[:, r:r + 1], (128, 128))
            l_in = jnp.broadcast_to(ft[:, g + r:g + r + 1], (128, 128))
            m_own = m_ref[at, :]
            m = jnp.maximum(m_own, m_in)
            w_own = jnp.exp2((m_own - m) * C2)
            w_in = jnp.exp2((m_in - m) * C2) * l_in
            total = acc_ref[at, 128:256] * w_own + w_in
            mixed = acc_ref[at, 0:128] * w_own + came[at, :].astype(F32) * w_in
            out_ref[at, :] = (mixed / jnp.maximum(total, 1e-35)).astype(BF16)
            m_ref[at, :] = m
            total_ref[at, :] = total
    else:
        total = acc_ref[:, 128:256]
        out_ref[0:ROWS, :] = (acc_ref[:, 0:128] / jnp.maximum(total, 1e-35)).astype(BF16)
        total_ref[...] = total

    compact = lambda x: jnp.sum(jnp.where(eye[None], x.reshape(g, 128, 128), 0.0), axis=1)
    stats = split3(compact(m_ref[...])) + split3(compact(total_ref[...]))
    pad = jnp.zeros((STAT - 6 * g, 128), F32)
    out_ref[ROWS:ROWS + STAT, :] = jnp.concatenate([x.astype(F32) for x in stats] + [pad], axis=0).astype(BF16)


def attend(hop, meta, q, kv_all, came):
    smem, vmem = pl.BlockSpec(memory_space=pltpu.SMEM), pl.BlockSpec(memory_space=pltpu.VMEM)
    tiles = 4 * kv_all[0].shape[2] // TILE
    came = [] if came is None else [came]
    return pl.pallas_call(
        functools.partial(attend_kernel, hop, bool(came)),
        out_shape=[jax.ShapeDtypeStruct((ROWS + STAT, 128), BF16), jax.ShapeDtypeStruct((12,), jnp.int32)],
        in_specs=[smem] + [vmem] * (4 + len(came)),
        out_specs=[vmem, smem],
        scratch_shapes=[
            pltpu.VMEM((tiles, ROWS, TILE), F32),
            pltpu.VMEM((ROWS, 256), F32),
            pltpu.VMEM((ROWS, 128), F32),
            pltpu.VMEM((ROWS, 256), F32),
            pltpu.VMEM((ROWS, 128), F32),
        ],
        compiler_params=pltpu.CompilerParams(vmem_limit_bytes=28 * MB),
        cost_estimate=pl.CostEstimate(flops=600_000_000, bytes_accessed=100_000, transcendentals=1_000),
        name="attend",
    )(meta, q, *kv_all, *came)


def combine_kernel(place, *refs):
    parts, (out_ref, *piece_refs, f_ref, flat_ref) = refs[:-7], refs[-7:]
    g = ROWS // 128
    ms, ls = zip(*[unpack_stats(ref[ROWS:ROWS + STAT, :].astype(F32)) for ref in parts])
    top = functools.reduce(jnp.maximum, ms)
    ws = [jnp.exp2((m - top) * C2) * l for m, l in zip(ms, ls)]
    whole = functools.reduce(jnp.add, ws)
    ft = columns(jnp.concatenate([w / whole for w in ws], axis=0))
    for r in range(g):
        total = jnp.zeros((128, 128), F32)
        for k, ref in enumerate(parts):
            total += ref[r * 128:(r + 1) * 128, :].astype(F32) * ft[:, k * g + r:k * g + r + 1]
        out_ref[r * 128:(r + 1) * 128, :] = total.astype(BF16)
        f_ref[r * 128:(r + 1) * 128, :] = total
    for h in range(8):
        flat_ref[:, h * 128:(h + 1) * 128] = f_ref[pl.ds(h, 64, stride=8), :].astype(BF16)
    core, xl = place[0], place[1]
    for i, ref in enumerate(piece_refs):
        c = core if i % 2 == 0 else 1 - core
        x = xl if i // 2 == 0 else 1 - xl
        ref[...] = flat_ref[pl.ds(pl.multiple_of(x * 32 + c * 16, 16), 16), :]


def combine(place, parts):
    vmem = pl.BlockSpec(memory_space=pltpu.VMEM)
    piece = jax.ShapeDtypeStruct((16, 1024), BF16)
    return pl.pallas_call(
        combine_kernel,
        out_shape=[jax.ShapeDtypeStruct((ROWS, 128), BF16)] + [piece] * 4,
        in_specs=[pl.BlockSpec(memory_space=pltpu.SMEM)] + [vmem] * len(parts),
        out_specs=[vmem] * 5,
        scratch_shapes=[pltpu.VMEM((ROWS, 128), F32), pltpu.VMEM((64, 1024), BF16)],
        compiler_params=pltpu.CompilerParams(vmem_limit_bytes=16 * MB),
        name="combine",
    )(place, *parts)


def local(queries, cache_keys, cache_values, span_keys, span_values, span_start, cache_lengths, out_weight):
    xl, z, y, xh, core = (lax.axis_index(a) for a in ("xl", "z", "y", "xh", "core"))
    sign = 1 - 2 * core
    kv = y * 2 + xh
    place = jnp.stack([core, xl, kv, z]).astype(jnp.int32)

    def shift(x, k):
        pairs = [(b * 2 + c, (b + k * (1 - 2 * c)) % NZ * 2 + c) for b in range(NZ) for c in range(2)]
        return lax.ppermute(x, ("z", "core"), pairs)

    swap = [(0, 1), (1, 0)]
    cross = [(i, 3 - i) for i in range(4)]
    mate = [(i, i ^ 1) for i in range(NZ)]

    both = [((a * NZ + b) * 2 + c, ((1 - a) * NZ + (b ^ 1)) * 2 + 1 - c) for a in range(2) for b in range(NZ) for c in range(2)]
    lengths = [
        cache_lengths,
        lax.ppermute(cache_lengths, ("xl", "xh"), cross),
        lax.ppermute(cache_lengths, "z", mate),
        lax.ppermute(cache_lengths, ("xl", "z", "xh"), both),
    ]

    near, far, rest = pack(place, cache_keys, cache_values, span_keys, span_values)
    near, far, lengths = lax.optimization_barrier((near, far, lengths))
    got_x = lax.ppermute(far, ("xl", "xh"), cross)
    got_z = lax.ppermute(near, "z", mate)

    q = payload(lengths, queries.reshape(ROWS, HD))
    q_blocks = [q, shift(q, 2), None, shift(q, -2)]
    got_z, q = lax.optimization_barrier((got_z, q))
    q_blocks[2] = shift(q_blocks[1], 2)
    got_zx = lax.ppermute(got_z, "xl", swap)
    got_x, got_z, got_zx, q_blocks[2], q_blocks[3], weight = lax.optimization_barrier(
        (got_x, got_z, got_zx, q_blocks[2], q_blocks[3], out_weight)
    )
    w_x1 = lax.ppermute(weight[0:768], "xl", swap)
    bufs = [near, rest]
    for got in (got_x, got_z, got_zx):
        bufs += [got, lax.ppermute(got, "core", swap)]
    *kv_all, meta = assemble(place, span_start, q_blocks, bufs)

    out, meta = attend(2, meta, q_blocks[2], kv_all, None)
    half_way = shift(out, 2)
    out, meta = attend(1, meta, q_blocks[1], kv_all, None)
    down = shift(out, -2)
    out, meta = attend(3, meta, q_blocks[3], kv_all, half_way)
    up = shift(out, 2)
    own, meta = attend(0, meta, q_blocks[0], kv_all, None)
    own, w_x1 = lax.optimization_barrier((own, w_x1))
    mixed, *pieces = combine(place, [own, up, down])
    attended = mixed.reshape(64, 8, HD)

    p_core = lax.ppermute(pieces[1], "core", swap)
    p_x = lax.ppermute(pieces[2], "xl", swap)
    p_both = lax.ppermute(pieces[3], ("xl", "core"), cross)
    p_core, p_x, p_both, weight = lax.optimization_barrier((p_core, p_x, p_both, weight))
    w_x2 = lax.ppermute(weight[768:1024], "xl", swap)
    w_core = lax.ppermute(weight, "core", swap)
    w_both1 = lax.ppermute(w_x1, "core", swap)
    w_both2 = lax.ppermute(w_x2, "core", swap)
    here = jnp.concatenate([pieces[0], p_core], axis=1)
    there = jnp.concatenate([p_x, p_both], axis=1)
    pair = jnp.stack([jnp.where(xl == 0, here, there), jnp.where(xl == 0, there, here)])[:, None]
    every = jnp.zeros((2, NZ, 16, 2048), BF16)
    every = lax.dynamic_update_slice(every, pair, (0, z, 0, 0))
    up = down = pair
    for k in range(1, 5):
        up = shift(up, 1)
        every = lax.dynamic_update_slice(every, up, (0, (z - sign * k + 2 * NZ) % NZ, 0, 0))
        if k < 4:
            down = shift(down, -1)
            every = lax.dynamic_update_slice(every, down, (0, (z + sign * k + 2 * NZ) % NZ, 0, 0))
    x = every.reshape(256, 2048)

    def term(*blocks):
        total, at = 0.0, 0
        for w in blocks:
            total = total + jnp.dot(x[:, at:at + w.shape[0]], w, preferred_element_type=F32)
            at += w.shape[0]
        return total.astype(BF16)

    t_own, t_peer = term(out_weight, w_core), term(w_x1, w_x2, w_both1, w_both2)
    terms = jnp.stack([jnp.where(xl == 0, t_own, t_peer), jnp.where(xl == 0, t_peer, t_own)])
    got = lax.all_to_all(terms.reshape(32, 16, 1024), ("xl", "y", "xh", "core"), 0, 0, tiled=True)
    projected = jnp.sum(got.reshape(2, 8, 2, 16, 1024).astype(F32), axis=1).astype(BF16).reshape(64, 1024)
    return attended, projected


def solution(mesh):
    fine = Mesh(mesh.devices.reshape(2, NZ, 4, 2, 2), ("xl", "z", "y", "xh", "core"))
    ctx, tp = ("xl", "z"), ("y", "xh", "core")
    return jax.shard_map(
        local,
        mesh=fine,
        in_specs=(
            P(ctx, tp, None),
            P(None, ctx, None),
            P(None, ctx, None),
            P(None, ctx, None),
            P(None, ctx, None),
            P(),
            P(ctx),
            P(tp, ctx),
        ),
        out_specs=(P(ctx, tp, None), P(tp, ctx)),
        check_vma=False,
    )
```

```python
import functools
import math

import jax
import jax.numpy as jnp
from jax import lax
from jax.experimental import pallas as pl
from jax.experimental.pallas import tpu as pltpu
from jax.sharding import Mesh, PartitionSpec as P

H = 128
KVH = 8
HD = 128
NEG = -1e30
SCALE = 1.0 / math.sqrt(HD)
C2 = math.log2(math.e) * SCALE
TILE = 256
ROWS = 512
STAT = 32
NZ = 8
SAFE = 90.0
F32 = jnp.float32
BF16 = jnp.bfloat16
MB = 1024 * 1024


def eye_mask():
    r = lax.broadcasted_iota(jnp.int32, (128, 128), 0)
    c = lax.broadcasted_iota(jnp.int32, (128, 128), 1)
    return r == c


def split3(x):
    hi = x.astype(BF16)
    rest = x - hi.astype(F32)
    mid = rest.astype(BF16)
    lo = (rest - mid.astype(F32)).astype(BF16)
    return hi, mid, lo


def pack_kernel(place, ck, cv, sk, sv, near_out, far_out, rest_out, hold, sem_in, sem_out):
    core, kv = place[0], place[2]
    n = ck.shape[1]
    step = n // 2

    def move(cache, span, cache2, span2):
        ins, outs = [], []
        for i, (src, tail, head, out) in enumerate(
            ((cache, span, kv, near_out), (cache, span, kv ^ 1, far_out), (cache2, span2, kv, rest_out))
        ):
            for j in range(3):
                at = pl.ds(j * step, step if j < 2 else 64)
                part = src.at[head, at] if j < 2 else tail.at[head]
                ins.append(pltpu.make_async_copy(part, hold.at[i, at], sem_in.at[i, j]))
                outs.append(pltpu.make_async_copy(hold.at[i, at], out.at[at], sem_out.at[i, j]))
        for c in ins:
            c.start()
        for c, d in zip(ins, outs):
            c.wait()
            d.start()
        for d in outs:
            d.wait()

    pl.when(core == 0)(lambda: move(ck, sk, cv, sv))
    pl.when(core == 1)(lambda: move(cv, sv, ck, sk))


def pack(place, ck, cv, sk, sv):
    n = ck.shape[1] + 64
    shape = jax.ShapeDtypeStruct((n, HD), BF16)
    anyspec = pl.BlockSpec(memory_space=pl.ANY)
    return pl.pallas_call(
        pack_kernel,
        out_shape=[shape] * 3,
        in_specs=[pl.BlockSpec(memory_space=pltpu.SMEM)] + [anyspec] * 4,
        out_specs=[anyspec] * 3,
        scratch_shapes=[
            pltpu.VMEM((3, n, HD), BF16),
            pltpu.SemaphoreType.DMA((3, 3)),
            pltpu.SemaphoreType.DMA((3, 3)),
        ],
        compiler_params=pltpu.CompilerParams(vmem_limit_bytes=57 * MB),
        name="pack",
    )(place, ck, cv, sk, sv)


def payload_kernel(own, x, z, zx, q_ref, out_ref):
    lens = [own[0], x[0], z[0], zx[0]]
    out_ref[0:ROWS, :] = q_ref[...]
    q = q_ref[...].astype(F32)
    norm = jnp.max(jnp.sum(q * q, axis=-1, keepdims=True), axis=0, keepdims=True)
    lane = lax.broadcasted_iota(jnp.int32, (16, 128), 1)
    row = jnp.where(lane == 8, norm * 1.02, 0.0)
    for i in range(4):
        row = jnp.where(lane == 2 * i, (lens[i] // 64).astype(F32), row)
        row = jnp.where(lane == 2 * i + 1, (lens[i] % 64).astype(F32), row)
    out_ref[ROWS:ROWS + 16, :] = row.astype(BF16)


def payload(lengths, q):
    smem, vmem = pl.BlockSpec(memory_space=pltpu.SMEM), pl.BlockSpec(memory_space=pltpu.VMEM)
    return pl.pallas_call(
        payload_kernel,
        out_shape=jax.ShapeDtypeStruct((ROWS + 16, HD), BF16),
        in_specs=[smem] * 4 + [vmem],
        out_specs=vmem,
        compiler_params=pltpu.CompilerParams(vmem_limit_bytes=8 * MB),
        name="payload",
    )(*lengths, q)


def assemble_kernel(place, start, *refs):
    qs, bufs, (kt_all, k_span, v_all, meta, k_all, sem) = refs[:4], refs[4:12], refs[12:]
    core, xl, z = place[0], place[1], place[3]
    sign = 1 - 2 * core
    firsts, seconds = bufs[0::2], bufs[1::2]

    def copies(keys, vals):
        pairs = [(k, k_all.at[i]) for i, k in enumerate(keys)] + [(v, v_all.at[i]) for i, v in enumerate(vals)]
        return [pltpu.make_async_copy(s, d, sem.at[i]) for i, (s, d) in enumerate(pairs)]

    def move(keys, vals):
        mine = copies(keys, vals)
        for c in mine:
            c.start()
        for c in mine:
            c.wait()

    pl.when(core == 0)(lambda: move(firsts, seconds))
    pl.when(core == 1)(lambda: move(seconds, firsts))

    lane = lax.broadcasted_iota(jnp.int32, (1, 128), 1)
    rows = [q[ROWS:ROWS + 16, :].astype(F32)[0:1, :] for q in qs]
    pick = lambda i: jnp.where(lane == 2 * i, 64.0, jnp.where(lane == 2 * i + 1, 1.0, 0.0))
    odd = lax.rem(z, 2)
    size = [jnp.sum(rows[0] * pick(i)) for i in range(4)]
    total = functools.reduce(jnp.add, rows)
    before = jnp.zeros((1, 128), F32)
    for j, row in enumerate(rows):
        at = lax.rem(z - 2 * sign * j + 2 * NZ, NZ)
        before += jnp.where(at < z, row, 0.0)
    sums = [jnp.sum(before * pick(i)) for i in range(4)]
    alls = [jnp.sum(total * pick(i)) for i in range(4)]
    low = jnp.where(xl == 0, alls[0] + alls[2], alls[1] + alls[3])
    for i in range(4):
        side, other = i % 2, i // 2
        pairs_before = sums[side] + sums[2 + side]
        own_odd = odd if other == 0 else 1 - odd
        mate = size[(2 - 2 * other) + side]
        offset = pairs_before + jnp.where(own_odd == 1, mate, 0.0)
        upper = xl if side == 0 else 1 - xl
        offset += jnp.where(upper == 1, low, 0.0)
        live = jnp.clip(start[0] - offset.astype(jnp.int32), 0, size[i].astype(jnp.int32))
        meta[i] = live
        zz = z if other == 0 else z + 1 - 2 * odd
        meta[4 + i] = (upper * NZ + zz) * 64
    meta[8] = z
    meta[9] = xl * 512
    meta[10] = sign
    q2 = jnp.sum(jnp.where(lane == 8, functools.reduce(jnp.maximum, rows), 0.0))
    n = kt_all.shape[2]
    k2 = jnp.zeros((1, n), F32)
    for i in range(4):
        kt = jnp.transpose(k_all[i, 0:n, :])
        kt_all[i] = kt
        kf = kt.astype(F32)
        k2 = jnp.maximum(k2, jnp.sum(kf * kf, axis=0, keepdims=True))
        tail = k_all[i, pl.ds(n, 64), :]
        k_span[i * 64:(i + 1) * 64, :] = tail
    tails = k_span[...].astype(F32)
    k2 = jnp.maximum(jnp.max(k2), jnp.max(jnp.sum(tails * tails, axis=-1, keepdims=True)))
    meta[11] = jnp.where(q2 * k2 * 1.04 <= (SAFE / C2) ** 2, 1, 0).astype(jnp.int32)


def assemble(place, start, qs, bufs):
    smem, vmem = pl.BlockSpec(memory_space=pltpu.SMEM), pl.BlockSpec(memory_space=pltpu.VMEM)
    n = bufs[0].shape[0]
    everything = jax.ShapeDtypeStruct((4, n, HD), BF16)
    turned = jax.ShapeDtypeStruct((4, HD, n - 64), BF16)
    tails = jax.ShapeDtypeStruct((256, HD), BF16)
    return pl.pallas_call(
        assemble_kernel,
        out_shape=[turned, tails, everything, jax.ShapeDtypeStruct((12,), jnp.int32)],
        in_specs=[smem, smem] + [vmem] * 4 + [pl.BlockSpec(memory_space=pl.ANY)] * 8,
        out_specs=[vmem, vmem, vmem, smem],
        scratch_shapes=[pltpu.VMEM((4, n, HD), BF16), pltpu.SemaphoreType.DMA((8,))],
        compiler_params=pltpu.CompilerParams(vmem_limit_bytes=24 * MB),
        name="assemble",
    )(place, start, *qs, *bufs)


def unpack_stats(st):
    g = ROWS // 128
    return st[0:g] + st[g:2 * g] + st[2 * g:3 * g], st[3 * g:4 * g] + st[4 * g:5 * g] + st[5 * g:6 * g]


def columns(rows):
    rows = jnp.concatenate([rows, jnp.zeros((128 - rows.shape[0], 128), F32)], axis=0)
    return jnp.transpose(rows)


def attend_kernel(hop, carried, meta, *refs):
    refs = list(refs)
    take = lambda n: [refs.pop(0) for _ in range(n)]
    q_ref, kt_all, k_span, v_all = take(4)
    came = take(1)[0] if carried else None
    out_ref, meta_out = take(2)
    s_ref, span_ref, m_ref, acc_ref, total_ref = refs
    for i in range(12):
        meta_out[i] = meta[i]
    z, base, sign, small = (meta[i] for i in range(8, 12))
    cache = kt_all.shape[2]
    ones = jnp.ones((256, 128), BF16)
    eye = eye_mask()
    g = ROWS // 128
    token0 = base + lax.rem(z - 2 * sign * hop + 2 * NZ, NZ) * 64

    def scores_of(turned):
        return jnp.dot(q_ref[0:ROWS, :], turned, preferred_element_type=F32)

    def span_scores():
        s = lax.dot_general(q_ref[0:ROWS, :], k_span[...], (((1,), (1,)), ((), ())), preferred_element_type=F32)
        col = lax.broadcasted_iota(jnp.int32, (1, 256), 1)
        owner = col // 64
        pos = col % 64
        for i in range(4):
            pos = jnp.where(owner == i, pos + meta[4 + i], pos)
        row = lax.broadcasted_iota(jnp.int32, s.shape, 0)
        return jnp.where(pos <= token0 + row // 8, s, NEG)

    def span_sums(p):
        values = jnp.concatenate([v_all[i, pl.ds(cache, 64), :] for i in range(4)], axis=0)
        return jnp.dot(p, jnp.concatenate([values, ones], axis=1), preferred_element_type=F32)

    @pl.when(small == 1)
    def _():
        acc_ref[...] = span_sums(jnp.exp(span_scores() * SCALE).astype(BF16))

        def shard(i, carry):
            live = meta[i]

            def piece(first, size, masked):
                def scores(j):
                    at = pl.ds(pl.multiple_of(first + j * 256, 256), 256)
                    return scores_of(kt_all[i, :, at])

                total = acc_ref[...]
                ahead = scores(0)
                for j in range(size // 256):
                    s = ahead * SCALE
                    if j + 1 < size // 256:
                        ahead = scores(j + 1)
                    if masked:
                        slot = first + j * 256 + lax.broadcasted_iota(jnp.int32, (1, 256), 1)
                        s = s + jnp.where(slot < live, 0.0, NEG)
                    p = jnp.exp(s).astype(BF16)
                    at = pl.ds(pl.multiple_of(first + j * 256, 256), 256)
                    v = jnp.concatenate([v_all[i, at, :], ones], axis=1)
                    total = total + jnp.dot(p, v, preferred_element_type=F32)
                acc_ref[...] = total

            def body(t, carry):
                piece(t * 1024, 1024, False)
                return carry

            whole = live // 1024
            first = whole * 1024
            n = (live - first + 255) // 256
            lax.fori_loop(0, whole, body, 0)

            def part(t, carry):
                piece(first + t * 512, 512, True)
                return carry

            lax.fori_loop(0, n // 2, part, 0)
            pl.when(n % 2 == 1)(lambda: piece(first + (n - 1) * 256, 256, True))
            return carry

        lax.fori_loop(0, 4, shard, 0)
        m_ref[...] = jnp.where(acc_ref[:, 128:256] > 0.0, 0.0, NEG)

    @pl.when(small == 0)
    def _():
        half = lambda x: functools.reduce(jnp.maximum, [x[:, j:j + 128] for j in range(0, x.shape[1], 128)])
        s = span_scores()
        span_ref[...] = s
        m_ref[...] = half(s)

        def score_shard(i, first):
            live = meta[i]
            tiles = (live + TILE - 1) // TILE

            def score(t, carry):
                at = pl.ds(pl.multiple_of(t * TILE, TILE), TILE)
                slot = t * TILE + lax.broadcasted_iota(jnp.int32, (1, TILE), 1)
                s = scores_of(kt_all[i, :, at]) + jnp.where(slot < live, 0.0, NEG)
                s_ref[first + t] = s
                m_ref[...] = jnp.maximum(m_ref[...], half(s))
                return carry

            lax.fori_loop(0, tiles, score, 0)
            return first + tiles

        lax.fori_loop(0, 4, score_shard, jnp.int32(0))
        m = jnp.broadcast_to(jnp.max(m_ref[...], axis=-1, keepdims=True), (ROWS, 128))
        m_ref[...] = m
        s = span_ref[...]
        wide = jnp.concatenate([m, m], axis=1)
        acc_ref[...] = span_sums(jnp.where(s > 0.5 * NEG, jnp.exp2((s - wide) * C2), 0.0).astype(BF16))

        def value_shard(i, first):
            tiles = (meta[i] + TILE - 1) // TILE

            def value(t, carry):
                at = pl.ds(pl.multiple_of(t * TILE, TILE), TILE)
                wide = jnp.concatenate([m_ref[...]] * (TILE // 128), axis=1)
                p = jnp.exp2((s_ref[first + t] - wide) * C2).astype(BF16)
                v = jnp.concatenate([v_all[i, at, :], ones], axis=1)
                acc_ref[...] += jnp.dot(p, v, preferred_element_type=F32)
                return carry

            lax.fori_loop(0, tiles, value, 0)
            return first + tiles

        lax.fori_loop(0, 4, value_shard, jnp.int32(0))

    if carried:
        ms, ls = unpack_stats(came[ROWS:ROWS + STAT, :].astype(F32))
        ft = columns(jnp.concatenate([ms, ls], axis=0))
        for r in range(g):
            at = slice(r * 128, (r + 1) * 128)
            m_in = jnp.broadcast_to(ft[:, r:r + 1], (128, 128))
            l_in = jnp.broadcast_to(ft[:, g + r:g + r + 1], (128, 128))
            m_own = m_ref[at, :]
            m = jnp.maximum(m_own, m_in)
            w_own = jnp.exp2((m_own - m) * C2)
            w_in = jnp.exp2((m_in - m) * C2) * l_in
            total = acc_ref[at, 128:256] * w_own + w_in
            mixed = acc_ref[at, 0:128] * w_own + came[at, :].astype(F32) * w_in
            out_ref[at, :] = (mixed / jnp.maximum(total, 1e-35)).astype(BF16)
            m_ref[at, :] = m
            total_ref[at, :] = total
    else:
        total = acc_ref[:, 128:256]
        out_ref[0:ROWS, :] = (acc_ref[:, 0:128] / jnp.maximum(total, 1e-35)).astype(BF16)
        total_ref[...] = total

    compact = lambda x: jnp.sum(jnp.where(eye[None], x.reshape(g, 128, 128), 0.0), axis=1)
    stats = split3(compact(m_ref[...])) + split3(compact(total_ref[...]))
    pad = jnp.zeros((STAT - 6 * g, 128), F32)
    out_ref[ROWS:ROWS + STAT, :] = jnp.concatenate([x.astype(F32) for x in stats] + [pad], axis=0).astype(BF16)


def attend(hop, meta, q, kv_all, came):
    smem, vmem = pl.BlockSpec(memory_space=pltpu.SMEM), pl.BlockSpec(memory_space=pltpu.VMEM)
    tiles = 4 * kv_all[0].shape[2] // TILE
    came = [] if came is None else [came]
    return pl.pallas_call(
        functools.partial(attend_kernel, hop, bool(came)),
        out_shape=[jax.ShapeDtypeStruct((ROWS + STAT, 128), BF16), jax.ShapeDtypeStruct((12,), jnp.int32)],
        in_specs=[smem] + [vmem] * (4 + len(came)),
        out_specs=[vmem, smem],
        scratch_shapes=[
            pltpu.VMEM((tiles, ROWS, TILE), F32),
            pltpu.VMEM((ROWS, 256), F32),
            pltpu.VMEM((ROWS, 128), F32),
            pltpu.VMEM((ROWS, 256), F32),
            pltpu.VMEM((ROWS, 128), F32),
        ],
        compiler_params=pltpu.CompilerParams(vmem_limit_bytes=28 * MB),
        cost_estimate=pl.CostEstimate(flops=600_000_000, bytes_accessed=100_000, transcendentals=1_000),
        name="attend",
    )(meta, q, *kv_all, *came)


def combine_kernel(place, *refs):
    parts, (out_ref, *piece_refs, f_ref, flat_ref) = refs[:-7], refs[-7:]
    g = ROWS // 128
    ms, ls = zip(*[unpack_stats(ref[ROWS:ROWS + STAT, :].astype(F32)) for ref in parts])
    top = functools.reduce(jnp.maximum, ms)
    ws = [jnp.exp2((m - top) * C2) * l for m, l in zip(ms, ls)]
    whole = functools.reduce(jnp.add, ws)
    ft = columns(jnp.concatenate([w / whole for w in ws], axis=0))
    for r in range(g):
        total = jnp.zeros((128, 128), F32)
        for k, ref in enumerate(parts):
            total += ref[r * 128:(r + 1) * 128, :].astype(F32) * ft[:, k * g + r:k * g + r + 1]
        out_ref[r * 128:(r + 1) * 128, :] = total.astype(BF16)
        f_ref[r * 128:(r + 1) * 128, :] = total
    for h in range(8):
        flat_ref[:, h * 128:(h + 1) * 128] = f_ref[pl.ds(h, 64, stride=8), :].astype(BF16)
    core, xl = place[0], place[1]
    for i, ref in enumerate(piece_refs):
        c = core if i % 2 == 0 else 1 - core
        x = xl if i // 2 == 0 else 1 - xl
        ref[...] = flat_ref[pl.ds(pl.multiple_of(x * 32 + c * 16, 16), 16), :]


def combine(place, parts):
    vmem = pl.BlockSpec(memory_space=pltpu.VMEM)
    piece = jax.ShapeDtypeStruct((16, 1024), BF16)
    return pl.pallas_call(
        combine_kernel,
        out_shape=[jax.ShapeDtypeStruct((ROWS, 128), BF16)] + [piece] * 4,
        in_specs=[pl.BlockSpec(memory_space=pltpu.SMEM)] + [vmem] * len(parts),
        out_specs=[vmem] * 5,
        scratch_shapes=[pltpu.VMEM((ROWS, 128), F32), pltpu.VMEM((64, 1024), BF16)],
        compiler_params=pltpu.CompilerParams(vmem_limit_bytes=16 * MB),
        name="combine",
    )(place, *parts)


def local(queries, cache_keys, cache_values, span_keys, span_values, span_start, cache_lengths, out_weight):
    xl, z, y, xh, core = (lax.axis_index(a) for a in ("xl", "z", "y", "xh", "core"))
    sign = 1 - 2 * core
    kv = y * 2 + xh
    place = jnp.stack([core, xl, kv, z]).astype(jnp.int32)

    def shift(x, k):
        pairs = [(b * 2 + c, (b + k * (1 - 2 * c)) % NZ * 2 + c) for b in range(NZ) for c in range(2)]
        return lax.ppermute(x, ("z", "core"), pairs)

    swap = [(0, 1), (1, 0)]
    cross = [(i, 3 - i) for i in range(4)]
    mate = [(i, i ^ 1) for i in range(NZ)]

    both = [((a * NZ + b) * 2 + c, ((1 - a) * NZ + (b ^ 1)) * 2 + 1 - c) for a in range(2) for b in range(NZ) for c in range(2)]
    lengths = [
        cache_lengths,
        lax.ppermute(cache_lengths, ("xl", "xh"), cross),
        lax.ppermute(cache_lengths, "z", mate),
        lax.ppermute(cache_lengths, ("xl", "z", "xh"), both),
    ]

    near, far, rest = pack(place, cache_keys, cache_values, span_keys, span_values)
    near, far, lengths = lax.optimization_barrier((near, far, lengths))
    got_x = lax.ppermute(far, ("xl", "xh"), cross)
    got_z = lax.ppermute(near, "z", mate)

    q = payload(lengths, queries.reshape(ROWS, HD))
    q_blocks = [q, shift(q, 2), None, shift(q, -2)]
    got_z, q = lax.optimization_barrier((got_z, q))
    q_blocks[2] = shift(q_blocks[1], 2)
    got_zx = lax.ppermute(got_z, "xl", swap)
    got_x, got_z, got_zx, q_blocks[2], q_blocks[3], weight = lax.optimization_barrier(
        (got_x, got_z, got_zx, q_blocks[2], q_blocks[3], out_weight)
    )
    w_x1 = lax.ppermute(weight[0:640], "xl", swap)
    bufs = [near, rest]
    for got in (got_x, got_z, got_zx):
        bufs += [got, lax.ppermute(got, "core", swap)]
    *kv_all, meta = assemble(place, span_start, q_blocks, bufs)

    out, meta = attend(2, meta, q_blocks[2], kv_all, None)
    half_way = shift(out, 2)
    out, meta = attend(1, meta, q_blocks[1], kv_all, None)
    down = shift(out, -2)
    out, meta = attend(3, meta, q_blocks[3], kv_all, half_way)
    up = shift(out, 2)
    own, meta = attend(0, meta, q_blocks[0], kv_all, None)
    own, w_x1 = lax.optimization_barrier((own, w_x1))
    mixed, *pieces = combine(place, [own, up, down])
    attended = mixed.reshape(64, 8, HD)

    p_core = lax.ppermute(pieces[1], "core", swap)
    p_x = lax.ppermute(pieces[2], "xl", swap)
    p_both = lax.ppermute(pieces[3], ("xl", "core"), cross)
    p_core, p_x, p_both, weight = lax.optimization_barrier((p_core, p_x, p_both, weight))
    w_x2 = lax.ppermute(weight[640:1024], "xl", swap)
    w_core = lax.ppermute(weight, "core", swap)
    w_both1 = lax.ppermute(w_x1, "core", swap)
    w_both2 = lax.ppermute(w_x2, "core", swap)
    here = jnp.concatenate([pieces[0], p_core], axis=1)
    there = jnp.concatenate([p_x, p_both], axis=1)
    pair = jnp.stack([jnp.where(xl == 0, here, there), jnp.where(xl == 0, there, here)])[:, None]
    every = jnp.zeros((2, NZ, 16, 2048), BF16)
    every = lax.dynamic_update_slice(every, pair, (0, z, 0, 0))
    up = down = pair
    for k in range(1, 5):
        up = shift(up, 1)
        every = lax.dynamic_update_slice(every, up, (0, (z - sign * k + 2 * NZ) % NZ, 0, 0))
        if k < 4:
            down = shift(down, -1)
            every = lax.dynamic_update_slice(every, down, (0, (z + sign * k + 2 * NZ) % NZ, 0, 0))
    x = every.reshape(256, 2048)

    def term(*blocks):
        total, at = 0.0, 0
        for w in blocks:
            total = total + jnp.dot(x[:, at:at + w.shape[0]], w, preferred_element_type=F32)
            at += w.shape[0]
        return total.astype(BF16)

    t_own, t_peer = term(out_weight, w_core), term(w_x1, w_x2, w_both1, w_both2)
    terms = jnp.stack([jnp.where(xl == 0, t_own, t_peer), jnp.where(xl == 0, t_peer, t_own)])
    got = lax.all_to_all(terms.reshape(32, 16, 1024), ("xl", "y", "xh", "core"), 0, 0, tiled=True)
    projected = jnp.sum(got.reshape(2, 8, 2, 16, 1024).astype(F32), axis=1).astype(BF16).reshape(64, 1024)
    return attended, projected


def solution(mesh):
    fine = Mesh(mesh.devices.reshape(2, NZ, 4, 2, 2), ("xl", "z", "y", "xh", "core"))
    ctx, tp = ("xl", "z"), ("y", "xh", "core")
    return jax.shard_map(
        local,
        mesh=fine,
        in_specs=(
            P(ctx, tp, None),
            P(None, ctx, None),
            P(None, ctx, None),
            P(None, ctx, None),
            P(None, ctx, None),
            P(),
            P(ctx),
            P(tp, ctx),
        ),
        out_specs=(P(ctx, tp, None), P(tp, ctx)),
        check_vma=False,
    )
```
